256 devices in a mesh: row: 8 (over z), col: 32 (over x, y, core).
Axes of the slice: x: 4, y: 4, z: 8, core: 2. Of those that a mesh axis runs over, the one named last changes fastest.
Arguments:
- a_values: bfloat16 [12288, 4096], P('row', 'col'), may hold values from 0 to 0.029907227
- b_values: bfloat16 [4096, 32768], P('col'), may hold values from 0 to 0.029907227
- a_pattern: int32 [96, 32], P('row', 'col'), may hold values 0 or 1
- b_pattern: int32 [32, 256], P('col'), may hold values 0 or 1
- c_pattern: int32 [96, 256], P('row', 'col'), may hold values 0 or 1
Outputs:
- rescaled: bfloat16 [12288, 32768], P('row', 'col')
The draws below stay inside these ranges and needn't reach their ends.
All inputs are finite; a program needn't handle non-finite values. No bound on the sum of `a_pattern` or of `b_pattern` or of `c_pattern` on one device may be relied on, other than what follows from the above.
Results may differ from the reference program's by a relative error of at most 0.001.
Values may be sent and summed in bfloat16 or wider, within the bound.
No kernel may reach another device: no remote copies, remote signals or barrier semaphores. Data moves between devices by JAX's collectives and lax.ppermute only.
A program may use at most 128 MiB of HBM per device.

```python
import jax
import jax.numpy as jnp

BLOCK = 128
NROWS = 12288
NINNER = 4096
NCOLS = 32768


def place_ends(entries, key, least, high):
    spot = [jax.random.randint(jax.random.fold_in(key, axis), (), 0, length) for axis, length in enumerate(entries.shape)]
    longest = entries.shape.index(max(entries.shape))
    neighbour = spot[:longest] + [(spot[longest] + 1) % entries.shape[longest]] + spot[longest + 1:]
    return entries.at[tuple(spot)].set(least).at[tuple(neighbour)].set(high)


def steps_of(stream_key, dims, split, smallest, top_value):
    gain, own = 1.0, jax.random.fold_in(stream_key, 6)
    for position, shards_of in split:
        steps = jnp.exp(jax.random.uniform(jax.random.fold_in(own, position), (shards_of,), jnp.float32, smallest / len(split), top_value / len(split)))
        gain = gain * jnp.repeat(steps, dims[position] // shards_of).reshape([-1 if axis == position else 1 for axis in range(len(dims))])
    return gain


def setup_inputs(seed: int = 0) -> dict:
    key_of = jax.random.split(jax.random.key(seed), 6)
    return {
        "a_values": jnp.clip(0.029907227 * jax.random.uniform(key_of[0], (NROWS, NINNER), jnp.float32) ** steps_of(key_of[0], (NROWS, NINNER), ((0, 8), (1, 32)), -0.2, 0.2), 0.0, 0.029907227).astype(jnp.bfloat16),
        "b_values": jnp.clip(0.029907227 * jax.random.uniform(key_of[1], (NINNER, NCOLS), jnp.float32) ** steps_of(key_of[1], (NINNER, NCOLS), ((0, 32),), -0.2, 0.2), 0.0, 0.029907227).astype(jnp.bfloat16),
        "a_pattern": place_ends((jax.random.randint(key_of[2], (NROWS // BLOCK, NINNER // BLOCK), 0, 2) < 1).astype(jnp.int32), jax.random.fold_in(key_of[2], 1), 0, 1),
        "b_pattern": place_ends((jax.random.randint(key_of[3], (NINNER // BLOCK, NCOLS // BLOCK), 0, 2) < 1).astype(jnp.int32), jax.random.fold_in(key_of[3], 1), 0, 1),
        "c_pattern": place_ends((jax.random.randint(key_of[4], (NROWS // BLOCK, NCOLS // BLOCK), 0, 4) < 3).astype(jnp.int32), jax.random.fold_in(key_of[4], 1), 0, 1),
    }


def expand_mask(values, pattern):
    row_count, col_count = pattern.shape
    shaped = values.reshape(row_count, BLOCK, col_count, BLOCK)
    masked = shaped * pattern.astype(values.dtype)[:, None, :, None]
    return masked.reshape(row_count * BLOCK, col_count * BLOCK)


def reference(a_values, b_values, a_pattern, b_pattern, c_pattern):
    left = expand_mask(a_values, a_pattern)
    right = expand_mask(b_values, b_pattern)
    expanded = jnp.dot(left, right, preferred_element_type=jnp.float32)
    expanded = expand_mask(expanded, c_pattern)
    inflated = expanded * expanded
    column_total = jnp.sum(inflated, axis=0)
    return (inflated * (NROWS / (column_total + 1e-6))[None, :]).astype(jnp.bfloat16)
```

```python
import functools

import jax
import jax.numpy as jnp
from jax import lax
from jax.experimental import pallas as pl
from jax.experimental.pallas import tpu as pltpu
from jax.sharding import PartitionSpec as P

BLOCK = 128
XS, YS, CORES = 4, 4, 2
COLS = XS * YS * CORES
ROWS = 8
EPS = 1e-06
F32 = jnp.float32
BF16 = jnp.bfloat16

OFFSETS = (0, -1, 1, 2)
NEAR = ((0, 0), (0, 1), (0, 2), (1, 0), (2, 0))
FAR = tuple((d, e) for d in range(4) for e in range(4) if (d, e) not in NEAR)
PAIRS = ((-1, 1), (-2, 2), (-3, 3), (0, 4))
TILE = 512


def flat(x, y, c):
    return ((x % XS) * YS + y % YS) * CORES + c


def place(x, y, c, first, second):
    if isinstance(c, int):
        return flat(x + first, y + second, c) if c == 0 else flat(x + second, y + first, c)
    dx = jnp.where(c == 0, first, second)
    dy = jnp.where(c == 0, second, first)
    return flat(x + dx + XS, y + dy + YS, c)


def shift(value, first, second):
    pairs = []
    for x in range(XS):
        for y in range(YS):
            for c in range(CORES):
                pairs.append((flat(x, y, c), place(x, y, c, first, second)))
    return lax.ppermute(value, "col", pairs)


def swap(value):
    return lax.ppermute(value, "col", [(i, i ^ 1) for i in range(COLS)])


def along(value, step):
    return lax.ppermute(value, "row", [(i, (i + step) % ROWS) for i in range(ROWS)])


def after(values, others):
    held, _ = lax.optimization_barrier((values, others))
    return held


def smem():
    return pl.BlockSpec(memory_space=pltpu.SMEM)


def vmem():
    return pl.BlockSpec(memory_space=pltpu.VMEM)


def any_space():
    return pl.BlockSpec(memory_space=pl.ANY)


def params():
    return pltpu.CompilerParams(vmem_limit_bytes=56 * 1024 * 1024)


def mask_left_kernel(pattern_ref, a_ref, o_ref):
    for i in range(a_ref.shape[0] // BLOCK):
        rows = slice(i * BLOCK, (i + 1) * BLOCK)
        block = a_ref[rows, :]
        o_ref[rows, :] = jnp.where(pattern_ref[i, 0] != 0, block, jnp.zeros_like(block))


def mask_left(a, pattern):
    return pl.pallas_call(
        mask_left_kernel,
        out_shape=jax.ShapeDtypeStruct(a.shape, a.dtype),
        in_specs=[smem(), vmem()],
        out_specs=vmem(),
        compiler_params=params(),
        cost_estimate=pl.CostEstimate(flops=a.size, bytes_accessed=4 * a.size, transcendentals=0),
    )(pattern, a)


def spread_kernel(row_ref, pattern_ref, b_ref, o_ref, held, sems):
    row = row_ref[0]
    count = o_ref.shape[0]

    def copy(j):
        columns = pl.ds(pl.multiple_of((j * ROWS + row) * BLOCK, BLOCK), BLOCK)
        return pltpu.make_async_copy(b_ref.at[:, columns], held.at[j], sems.at[j])

    for j in range(count):
        copy(j).start()
    for j in range(count):
        copy(j).wait()
        block = held[j]
        o_ref[j] = jnp.where(pattern_ref[0, j * ROWS + row] != 0, block, jnp.zeros_like(block))


def spread(b, pattern, row):
    shape = (COLS, b.shape[0], BLOCK)
    return pl.pallas_call(
        spread_kernel,
        out_shape=jax.ShapeDtypeStruct(shape, b.dtype),
        in_specs=[smem(), smem(), any_space()],
        out_specs=vmem(),
        scratch_shapes=[pltpu.VMEM(shape, b.dtype), pltpu.SemaphoreType.DMA((COLS,))],
        compiler_params=params(),
        cost_estimate=pl.CostEstimate(flops=1 << 20, bytes_accessed=1 << 21, transcendentals=0),
    )(row, pattern, b)


def pieces_kernel(where_ref, pattern_ref, b_ref, *rest):
    outs, held, sems = rest[:5], rest[5], rest[6]
    width = outs[0].shape[2]
    blocks = width // BLOCK

    def copy(k):
        columns = pl.ds(pl.multiple_of(where_ref[k] * width, width), width)
        return pltpu.make_async_copy(b_ref.at[:, columns], held.at[k], sems.at[k])

    for k in range(10):
        copy(k).start()
    for k in range(10):
        copy(k).wait()
        for i in range(blocks):
            columns = slice(i * BLOCK, (i + 1) * BLOCK)
            block = held[k, :, columns]
            keep = pattern_ref[0, where_ref[k] * blocks + i] != 0
            outs[k // 2][k % 2, :, columns] = jnp.where(keep, block, jnp.zeros_like(block))


def pieces(b, pattern, where):
    width = b.shape[1] // COLS
    shape = (2, b.shape[0], width)
    return pl.pallas_call(
        pieces_kernel,
        out_shape=[jax.ShapeDtypeStruct(shape, b.dtype)] * 5,
        in_specs=[smem(), smem(), any_space()],
        out_specs=[vmem()] * 5,
        scratch_shapes=[pltpu.VMEM((10, b.shape[0], width), b.dtype), pltpu.SemaphoreType.DMA((10,))],
        compiler_params=params(),
        cost_estimate=pl.CostEstimate(flops=3 << 20, bytes_accessed=6 << 20, transcendentals=0),
    )(where, pattern, b)


def select_kernel(index_ref, r_ref, o_ref, sem):
    for j in range(o_ref.shape[0]):
        pltpu.make_async_copy(r_ref.at[index_ref[j]], o_ref.at[j], sem.at[j]).start()
    for j in range(o_ref.shape[0]):
        pltpu.make_async_copy(r_ref.at[index_ref[j]], o_ref.at[j], sem.at[j]).wait()


def select(received, index):
    count = index.shape[0]
    return pl.pallas_call(
        select_kernel,
        out_shape=jax.ShapeDtypeStruct((count,) + received.shape[1:], received.dtype),
        in_specs=[smem(), any_space()],
        out_specs=any_space(),
        scratch_shapes=[pltpu.SemaphoreType.DMA((count,))],
        compiler_params=params(),
        cost_estimate=pl.CostEstimate(flops=0, bytes_accessed=2 << 20, transcendentals=0),
    )(index, received)


def product_kernel(far_counts, last, blk_ref, cpat_ref, *refs):
    refs = list(refs)
    lefts = [refs.pop(0) for _ in range(8)]
    nears = [[refs.pop(0) for _ in range(6)] for _ in range(2)]
    fars = [[refs.pop(0) for _ in range(n)] for n in far_counts]
    earlier = [refs.pop(0) for _ in range(3)] if last else []
    o_ref, t_ref = refs.pop(0), refs.pop(0)
    right = refs.pop(0)
    step = pl.program_id(0)

    @pl.when(step == 0)
    def _():
        for n in range(2):
            lanes = slice(n * BLOCK, (n + 1) * BLOCK)
            for o in range(2):
                for k, (d, e) in enumerate(NEAR):
                    slot = (o * 4 + d) * 4 + e
                    block = nears[n][k][...] if o == 0 else nears[n][5][k]
                    right[slot * BLOCK:(slot + 1) * BLOCK, lanes] = block
                for k, (d, e) in enumerate(FAR):
                    slot = (o * 4 + d) * 4 + e
                    if len(fars[n]) == 1:
                        block = fars[n][0][o * len(FAR) + k]
                    else:
                        block = fars[n][o][k]
                    right[slot * BLOCK:(slot + 1) * BLOCK, lanes] = block

    left = jnp.concatenate([ref[e] for ref in lefts for e in range(4)], axis=1)
    product = jnp.dot(left, right[...], preferred_element_type=F32)
    blocks = TILE // BLOCK
    sums = [jnp.zeros((1, BLOCK), F32) for _ in range(2)]
    for n in range(2):
        lanes = slice(n * BLOCK, (n + 1) * BLOCK)
        for i in range(blocks):
            rows = slice(i * BLOCK, (i + 1) * BLOCK)
            keep = cpat_ref[step * blocks + i, blk_ref[n]] != 0
            block = product[rows, lanes]
            block = jnp.where(keep, block * block, jnp.zeros_like(block))
            o_ref[rows, lanes] = block
            sums[n] = sums[n] + jnp.sum(block, axis=0, keepdims=True)

    if not last:
        @pl.when(step == 0)
        def _():
            t_ref[...] = jnp.zeros_like(t_ref)

        for n in range(2):
            t_ref[n:n + 1, :] += sums[n]
    else:
        total = refs.pop(0)

        @pl.when(step == 0)
        def _():
            total[...] = jnp.zeros_like(total)

        for n in range(2):
            total[n:n + 1, :] += sums[n]

        @pl.when(step == pl.num_programs(0) - 1)
        def _():
            for k in range(ROWS):
                source = earlier[k // 2] if k < 6 else total
                n = k % 2
                where = blk_ref[2 + k]
                for r in range(ROWS):
                    t_ref[r, pl.ds(where, 1), :] = source[n:n + 1, :]


def product(blk, cpat, lefts, near, nears, fars, earlier=None, everywhere=None):
    last = earlier is not None
    rows = lefts[0].shape[1]
    scalars = blk if not last else jnp.concatenate([blk, everywhere])
    in_specs = [pl.BlockSpec((4, TILE, BLOCK), lambda i, *_: (0, i, 0)) for _ in lefts]
    operands = list(lefts)
    for n in range(2):
        for array in nears:
            in_specs.append(pl.BlockSpec((None, BLOCK, BLOCK), lambda i, s, _, n=n: (0, 0, s[n])))
            operands.append(array)
        in_specs.append(pl.BlockSpec((5, BLOCK, BLOCK), lambda i, s, _, n=n: (0, 0, s[n])))
        operands.append(near)
    for group in fars:
        for array in group:
            in_specs.append(pl.BlockSpec(array.shape, lambda i, *_: (0, 0, 0)))
            operands.append(array)
    out_shape = [jax.ShapeDtypeStruct((rows, 2 * BLOCK), F32)]
    out_specs = [pl.BlockSpec((TILE, 2 * BLOCK), lambda i, *_: (i, 0))]
    scratch = [pltpu.VMEM((COLS * BLOCK, 2 * BLOCK), BF16)]
    if last:
        for array in earlier:
            in_specs.append(pl.BlockSpec(array.shape, lambda i, *_: (0, 0)))
            operands.append(array)
        out_shape.append(jax.ShapeDtypeStruct((ROWS, ROWS, BLOCK), F32))
        out_specs.append(pl.BlockSpec((ROWS, ROWS, BLOCK), lambda i, *_: (0, 0, 0)))
        scratch.append(pltpu.VMEM((2, BLOCK), F32))
    else:
        out_shape.append(jax.ShapeDtypeStruct((2, BLOCK), F32))
        out_specs.append(pl.BlockSpec((2, BLOCK), lambda i, *_: (0, 0)))
    return pl.pallas_call(
        functools.partial(product_kernel, tuple(len(g) for g in fars), last),
        out_shape=out_shape,
        grid_spec=pltpu.PrefetchScalarGridSpec(
            num_scalar_prefetch=2,
            grid=(rows // TILE,),
            in_specs=in_specs,
            out_specs=out_specs,
            scratch_shapes=scratch,
        ),
        compiler_params=params(),
        cost_estimate=pl.CostEstimate(
            flops=2 * rows * COLS * BLOCK * 2 * BLOCK, bytes_accessed=16 << 20, transcendentals=0
        ),
    )(scalars, cpat, *operands)


def rescale_kernel(count, blk_ref, t_ref, i0, i1, i2, i3, o_ref, scale):
    total = t_ref[0]
    for r in range(1, ROWS):
        total = total + t_ref[r]
    scale[...] = count / (total + EPS)
    for k, ref in enumerate((i0, i1, i2, i3)):
        for n in range(2):
            where = blk_ref[2 * k + n]
            lanes = pl.ds(pl.multiple_of(where * BLOCK, BLOCK), BLOCK)
            factor = scale[pl.ds(where, 1), :]
            o_ref[:, lanes] = (ref[:, n * BLOCK:(n + 1) * BLOCK] * factor).astype(BF16)


def rescale(everywhere, totals, inflated):
    rows = inflated[0].shape[0]
    return pl.pallas_call(
        functools.partial(rescale_kernel, float(rows * ROWS)),
        out_shape=jax.ShapeDtypeStruct((rows, ROWS * BLOCK), BF16),
        grid_spec=pltpu.PrefetchScalarGridSpec(
            num_scalar_prefetch=1,
            grid=(rows // TILE,),
            in_specs=[pl.BlockSpec(totals.shape, lambda i, *_: (0, 0, 0))]
            + [pl.BlockSpec((TILE, 2 * BLOCK), lambda i, *_: (i, 0))] * 4,
            out_specs=pl.BlockSpec((TILE, ROWS * BLOCK), lambda i, *_: (i, 0)),
            scratch_shapes=[pltpu.VMEM((ROWS, BLOCK), F32)],
        ),
        compiler_params=params(),
        cost_estimate=pl.CostEstimate(flops=rows * 2048, bytes_accessed=10 << 20, transcendentals=0),
    )(everywhere, totals, *inflated)


def shards(a_values, b_values, a_pattern, b_pattern, c_pattern):
    col = lax.axis_index("col").astype(jnp.int32)
    row = lax.axis_index("row").astype(jnp.int32)
    x, y, c = col // (YS * CORES), (col // CORES) % YS, col % CORES

    sent = spread(b_values, b_pattern, row[None])
    received = lax.all_to_all(sent, "col", split_axis=0, concat_axis=0, tiled=True)

    left = mask_left(a_values, a_pattern)[None]
    line = [left] + [shift(left, s, 0) for s in (1, -1, 2)]

    index = []
    for core in (c, 1 - c):
        for d, e in FAR:
            index.append(place(x, y, core, OFFSETS[e], OFFSETS[d]))
    own = select(received, jnp.stack(index))

    up, down = [own], [own]
    for _ in range(3):
        up.append(along(up[-1], 1))
        down.append(along(down[-1], -1))
    half = len(FAR)
    opposite = [along(up[-1][:half], 1), along(down[-1][half:], -1)]

    line = jnp.concatenate(line, axis=0)
    lefts = [line] + [shift(line, 0, s) for s in (1, -1, 2)]
    lefts = lefts + [swap(g) for g in lefts]

    where = []
    for first, second in ((0, 0), (1, 0), (-1, 0), (0, 1), (0, -1)):
        there = place(x, y, c, first, second)
        where += [there, there ^ 1]
    near = pieces(after(b_values, own), b_pattern, jnp.stack(where))
    nears = [near[0], shift(near[1], 1, 0), shift(near[2], -1, 0), shift(near[3], 0, 1), shift(near[4], 0, -1)]
    other = swap(jnp.stack([piece[1] for piece in nears]))

    blocks = [[(row + ROWS + k) % ROWS for k in pair] for pair in PAIRS]
    everywhere = jnp.stack([b for pair in blocks for b in pair])
    inflated, totals = [], []
    for k in range(3):
        out, total = product(jnp.stack(blocks[k]), c_pattern, lefts, other, nears, [[up[k + 1]], [down[k + 1]]])
        inflated.append(out)
        totals.append(total)
    out, total = product(
        jnp.stack(blocks[3]), c_pattern, lefts, other, nears, [[own], opposite], totals, everywhere
    )
    inflated.append(out)
    gathered = lax.all_to_all(total, "row", split_axis=0, concat_axis=0, tiled=True)
    return rescale(everywhere, gathered, inflated)


def solution(mesh):
    return jax.shard_map(
        shards,
        mesh=mesh,
        in_specs=(
            P("row", "col"),
            P("col", None),
            P("row", "col"),
            P("col", None),
            P("row", "col"),
        ),
        out_specs=P("row", "col"),
        check_vma=False,
    )
```

```python
import functools

import jax
import jax.numpy as jnp
from jax import lax
from jax.experimental import pallas as pl
from jax.experimental.pallas import tpu as pltpu
from jax.sharding import PartitionSpec as P

BLOCK = 128
XS, YS, CORES = 4, 4, 2
COLS = XS * YS * CORES
ROWS = 8
EPS = 1e-06
F32 = jnp.float32
BF16 = jnp.bfloat16

OFFSETS = (0, -1, 1, 2)
NEAR = ((0, 0), (0, 1), (0, 2), (1, 0), (2, 0))
FAR = tuple((d, e) for d in range(4) for e in range(4) if (d, e) not in NEAR)


def flat(x, y, c):
    return ((x & (XS - 1)) * YS + (y & (YS - 1))) * CORES + c


def place(x, y, c, first, second):
    if isinstance(c, int):
        return flat(x + first, y + second, c) if c == 0 else flat(x + second, y + first, c)
    dx = jnp.where(c == 0, first, second)
    dy = jnp.where(c == 0, second, first)
    return flat(x + dx, y + dy, c)


def shift(value, first, second):
    pairs = []
    for x in range(XS):
        for y in range(YS):
            for c in range(CORES):
                pairs.append((flat(x, y, c), place(x, y, c, first, second)))
    return lax.ppermute(value, "col", pairs)


def swap(value):
    return lax.ppermute(value, "col", [(i, i ^ 1) for i in range(COLS)])


def smem():
    return pl.BlockSpec(memory_space=pltpu.SMEM)


def vmem():
    return pl.BlockSpec(memory_space=pltpu.VMEM)


def any_space():
    return pl.BlockSpec(memory_space=pl.ANY)


def params():
    return pltpu.CompilerParams(vmem_limit_bytes=56 * 1024 * 1024)


def mask_left_kernel(pattern_ref, a_ref, o_ref):
    for i in range(a_ref.shape[0] // BLOCK):
        rows = slice(i * BLOCK, (i + 1) * BLOCK)
        block = a_ref[rows, :]
        o_ref[rows, :] = jnp.where(pattern_ref[i, 0] != 0, block, jnp.zeros_like(block))


def mask_left(a, pattern):
    return pl.pallas_call(
        mask_left_kernel,
        out_shape=jax.ShapeDtypeStruct(a.shape, a.dtype),
        in_specs=[smem(), vmem()],
        out_specs=vmem(),
        compiler_params=params(),
        cost_estimate=pl.CostEstimate(flops=a.size, bytes_accessed=4 * a.size, transcendentals=0),
    )(pattern, a)


def spread_kernel(row_ref, pattern_ref, b_ref, o_ref, held, sems):
    row = row_ref[0]
    count = o_ref.shape[0]

    def copy(j):
        columns = pl.ds(pl.multiple_of((j * ROWS + row) * BLOCK, BLOCK), BLOCK)
        return pltpu.make_async_copy(b_ref.at[:, columns], held.at[j], sems.at[j])

    for j in range(count):
        copy(j).start()
    for j in range(count):
        copy(j).wait()
        block = held[j]
        o_ref[j] = jnp.where(pattern_ref[0, j * ROWS + row] != 0, block, jnp.zeros_like(block))


def spread(b, pattern, row):
    shape = (COLS, b.shape[0], BLOCK)
    return pl.pallas_call(
        spread_kernel,
        out_shape=jax.ShapeDtypeStruct(shape, b.dtype),
        in_specs=[smem(), smem(), any_space()],
        out_specs=vmem(),
        scratch_shapes=[pltpu.VMEM(shape, b.dtype), pltpu.SemaphoreType.DMA((COLS,))],
        compiler_params=params(),
        cost_estimate=pl.CostEstimate(flops=1 << 20, bytes_accessed=1 << 21, transcendentals=0),
    )(row, pattern, b)


def pieces_kernel(where_ref, pattern_ref, b_ref, *rest):
    count = len(NEAR)
    outs, held, sems = rest[:count], rest[count], rest[count + 1]
    width = outs[0].shape[2]
    blocks = width // BLOCK

    def copy(k):
        columns = pl.ds(pl.multiple_of(where_ref[k] * width, width), width)
        return pltpu.make_async_copy(b_ref.at[:, columns], held.at[k], sems.at[k])

    for k in range(2 * count):
        copy(k).start()
    for k in range(2 * count):
        copy(k).wait()
        for i in range(blocks):
            columns = slice(i * BLOCK, (i + 1) * BLOCK)
            block = held[k, :, columns]
            keep = pattern_ref[0, where_ref[k] * blocks + i] != 0
            outs[k // 2][k % 2, :, columns] = jnp.where(keep, block, jnp.zeros_like(block))


def pieces(b, pattern, where):
    width, count = b.shape[1] // COLS, len(NEAR)
    shape = (2, b.shape[0], width)
    return pl.pallas_call(
        pieces_kernel,
        out_shape=[jax.ShapeDtypeStruct(shape, b.dtype)] * count,
        in_specs=[smem(), smem(), any_space()],
        out_specs=[vmem()] * count,
        scratch_shapes=[
            pltpu.VMEM((2 * count, b.shape[0], width), b.dtype),
            pltpu.SemaphoreType.DMA((2 * count,)),
        ],
        compiler_params=params(),
        cost_estimate=pl.CostEstimate(flops=4 << 20, bytes_accessed=8 << 20, transcendentals=0),
    )(where, pattern, b)


def select_kernel(index_ref, r_ref, o_ref):
    for j in range(o_ref.shape[0]):
        o_ref[j] = r_ref[index_ref[j]]


def select(received, index):
    count = index.shape[0]
    return pl.pallas_call(
        select_kernel,
        out_shape=jax.ShapeDtypeStruct((count,) + received.shape[1:], received.dtype),
        in_specs=[smem(), vmem()],
        out_specs=vmem(),
        compiler_params=params(),
        cost_estimate=pl.CostEstimate(flops=0, bytes_accessed=2 << 20, transcendentals=0),
    )(index, pltpu.with_memory_space_constraint(received, pltpu.HBM))


CHUNK, TILE = 384, 512
HALF = 768


def held(value):
    return pltpu.with_memory_space_constraint(value, pltpu.VMEM)


def limit(size):
    return pltpu.CompilerParams(vmem_limit_bytes=size << 20)


def runs(o, d):
    found = []
    for e in range(4):
        if (d, e) in FAR:
            spot = o * len(FAR) + FAR.index((d, e))
        else:
            spot = 2 * len(FAR) + o * len(NEAR) + NEAR.index((d, e))
        if found and found[-1][2] + found[-1][1] == spot:
            found[-1][1] += 1
        else:
            found.append([e, 1, spot])
    return found


def near_kernel(*refs):
    refs = list(refs)
    lefts = [refs.pop(0) for _ in range(10)]
    nears = [refs.pop(0) for _ in range(len(NEAR) + 1)]
    left_out, o_ref, left, piece, near, out, nsem, lsem, osem = refs
    rows, count, depth = o_ref.shape[0], len(NEAR), left_out.shape[1]

    whole = [pltpu.make_async_copy(nears[k].at[0], near.at[k], nsem.at[k]) for k in range(count)]
    whole.append(pltpu.make_async_copy(nears[count], near.at[pl.ds(count, count)], nsem.at[count]))
    parts = []
    for i in range(rows // CHUNK):
        start = i * CHUNK
        part = []
        for k in range(8):
            o, d = k // 4, k % 4
            if d < 3:
                source = lefts[o * 5 + d].at[pl.ds(start, CHUNK), :]
            else:
                source = lefts[o * 5 + 3 + start // HALF].at[pl.ds(start % HALF, CHUNK), :]
            part.append(pltpu.make_async_copy(source, piece.at[i % 2, k], lsem.at[i * 8 + k]))
        parts.append(part)
    for group in (parts[0], whole, parts[1]):
        for copy in group:
            copy.start()
    outs = []
    for i, part in enumerate(parts):
        here, slot = pl.ds(i * CHUNK, CHUNK), i % 2
        for copy in part:
            copy.wait()
        if i >= 2:
            for copy in outs[i - 2]:
                copy.wait()
        for k in range(8):
            for block, width, spot in runs(k // 4, k % 4):
                lanes = slice(block * BLOCK, (block + width) * BLOCK)
                target = slice(spot * BLOCK, (spot + width) * BLOCK)
                left[slot, :, target] = piece[slot, k, :, lanes]
        if i + 2 < len(parts):
            for copy in parts[i + 2]:
                copy.start()
        outs.append([
            pltpu.make_async_copy(left.at[slot, :, pl.ds(0, depth)], left_out.at[here, :], osem.at[2 * i]),
            pltpu.make_async_copy(out.at[slot], o_ref.at[here, :], osem.at[2 * i + 1]),
        ])
        outs[i][0].start()
        if i == 0:
            for copy in whole:
                copy.wait()
        out[slot] = jnp.dot(
            left[slot, :, depth:],
            near[...].reshape(2 * count * BLOCK, ROWS * BLOCK),
            preferred_element_type=F32,
        )
        outs[i][1].start()
    for pair in outs[-2:]:
        for copy in pair:
            copy.wait()


def far_kernel(cpat_ref, left_in, sum_in, fars, o_ref, t_ref, left, partial, far, fsem, lsem):
    rows, sources = o_ref.shape[0], 2 * len(FAR)
    depth = sources * BLOCK
    blocks = [
        pltpu.make_async_copy(
            fars.at[pl.ds(n * sources, sources)],
            far.at[n // 2, :, :, pl.ds(n % 2 * BLOCK, BLOCK)],
            fsem.at[n],
        )
        for n in range(ROWS)
    ]
    parts = []
    for i in range(rows // CHUNK):
        here = pl.ds(i * CHUNK, CHUNK)
        parts.append([
            pltpu.make_async_copy(left_in.at[here, :], left.at[here, :], lsem.at[2 * i]),
            pltpu.make_async_copy(sum_in.at[here, :], partial.at[here, :], lsem.at[2 * i + 1]),
        ])
    for group in (blocks[:2], parts[0], blocks[2:4], *parts[1:], blocks[4:]):
        for copy in group:
            copy.start()
    sums = [jnp.zeros((1, BLOCK), F32) for _ in range(ROWS)]

    def multiply(pair, start, size):
        product = jnp.dot(
            left[start:start + size, :], far[pair].reshape(depth, 2 * BLOCK), preferred_element_type=F32
        )
        for n in range(2):
            lanes = slice(n * BLOCK, (n + 1) * BLOCK)
            column = 2 * pair + n
            target = slice(column * BLOCK, (column + 1) * BLOCK)
            for j in range(size // BLOCK):
                keep = cpat_ref[start // BLOCK + j, column] != 0
                place = slice(start + j * BLOCK, start + (j + 1) * BLOCK)
                block = product[j * BLOCK:(j + 1) * BLOCK, lanes] + partial[place, target]
                block = jnp.where(keep, block * block, jnp.zeros_like(block))
                o_ref[place, target] = block
                sums[column] = sums[column] + jnp.sum(block, axis=0, keepdims=True)

    for copy in blocks[:2]:
        copy.wait()
    for i, part in enumerate(parts):
        for copy in part:
            copy.wait()
        multiply(0, i * CHUNK, CHUNK)
        if i == 0:
            for copy in blocks[2:4]:
                copy.wait()
        multiply(1, i * CHUNK, CHUNK)
    for pair in (2, 3):
        for copy in blocks[2 * pair:2 * pair + 2]:
            copy.wait()
        for start in range(0, rows, TILE):
            multiply(pair, start, TILE)
    for r in range(ROWS):
        for n in range(ROWS):
            t_ref[r, n:n + 1, :] = sums[n]


def cost(rows, sources, data):
    return pl.CostEstimate(
        flops=2 * rows * sources * BLOCK * ROWS * BLOCK, bytes_accessed=data << 20, transcendentals=0
    )


def near_product(lefts, nears):
    rows = 2 * HALF
    return pl.pallas_call(
        near_kernel,
        out_shape=[
            jax.ShapeDtypeStruct((rows, 2 * len(FAR) * BLOCK), BF16),
            jax.ShapeDtypeStruct((rows, ROWS * BLOCK), F32),
        ],
        in_specs=[any_space()] * (len(lefts) + len(nears)),
        out_specs=[any_space()] * 2,
        scratch_shapes=[
            pltpu.VMEM((2, CHUNK, COLS * BLOCK), BF16),
            pltpu.VMEM((2, 8, CHUNK, 512), BF16),
            pltpu.VMEM((2 * len(NEAR), BLOCK, ROWS * BLOCK), BF16),
            pltpu.VMEM((2, CHUNK, ROWS * BLOCK), F32),
            pltpu.SemaphoreType.DMA((len(nears),)),
            pltpu.SemaphoreType.DMA((32,)),
            pltpu.SemaphoreType.DMA((8,)),
        ],
        compiler_params=limit(24),
        cost_estimate=cost(rows, 2 * len(NEAR), 32),
    )(*lefts, *nears)


def far_product(cpat, left, partial, fars):
    rows, depth = left.shape
    left, partial, fars = [
        pltpu.with_memory_space_constraint(array, pltpu.HBM) for array in (left, partial, fars)
    ]
    return pl.pallas_call(
        far_kernel,
        out_shape=[
            pltpu.VMEM((rows, ROWS * BLOCK), F32),
            jax.ShapeDtypeStruct((ROWS, ROWS, BLOCK), F32),
        ],
        in_specs=[smem()] + [any_space()] * 3,
        out_specs=[vmem()] * 2,
        scratch_shapes=[
            pltpu.VMEM((rows, depth), BF16),
            pltpu.VMEM((rows, ROWS * BLOCK), F32),
            pltpu.VMEM((ROWS // 2, 2 * len(FAR), BLOCK, 2 * BLOCK), BF16),
            pltpu.SemaphoreType.DMA((ROWS,)),
            pltpu.SemaphoreType.DMA((8,)),
        ],
        compiler_params=limit(32),
        cost_estimate=cost(rows, 2 * len(FAR), 24),
    )(cpat, left, partial, fars)


def rescale_kernel(count, t_ref, i_ref, o_ref):
    total = t_ref[0]
    for r in range(1, ROWS):
        total = total + t_ref[r]
    scale = count / (total + EPS)
    rows = pl.ds(pl.program_id(0) * o_ref.shape[0], o_ref.shape[0])
    for n in range(ROWS):
        lanes = slice(n * BLOCK, (n + 1) * BLOCK)
        o_ref[:, lanes] = (i_ref[rows, lanes] * scale[n:n + 1, :]).astype(BF16)


def rescale(totals, inflated):
    rows, columns = inflated.shape
    tile = 256
    return pl.pallas_call(
        functools.partial(rescale_kernel, float(rows * ROWS)),
        out_shape=jax.ShapeDtypeStruct((rows, columns), BF16),
        grid=(rows // tile,),
        in_specs=[pl.BlockSpec(totals.shape, lambda i: (0, 0, 0)), vmem()],
        out_specs=pl.BlockSpec((tile, columns), lambda i: (i, 0)),
        compiler_params=limit(16),
        cost_estimate=pl.CostEstimate(flops=rows * 2048, bytes_accessed=4 << 20, transcendentals=0),
    )(totals, held(inflated))


def shards(a_values, b_values, a_pattern, b_pattern, c_pattern):
    col = lax.axis_index("col").astype(jnp.int32)
    row = lax.axis_index("row").astype(jnp.int32)
    x, y, c = col >> 3, (col >> 1) & (YS - 1), col & (CORES - 1)

    sent = spread(b_values, b_pattern, row[None])
    received = lax.all_to_all(sent, "col", split_axis=0, concat_axis=0, tiled=True)

    left = mask_left(a_values, a_pattern)
    where = []
    steps = ((0, 0), (1, 0), (-1, 0), (0, 1), (0, -1))
    for first, second in steps:
        there = place(x, y, c, first, second)
        where += [there, there ^ 1]
    near = pieces(b_values, b_pattern, jnp.stack(where))
    index = []
    for core in (c, 1 - c):
        for d, e in FAR:
            index.append(place(x, y, core, OFFSETS[e], OFFSETS[d]))
    received, left, near = lax.optimization_barrier((received, left, near))
    own = select(received, jnp.stack(index))
    left, near, _ = lax.optimization_barrier((left, near, own))

    fars = lax.all_gather(own, "row", axis=0, tiled=True)

    line = jnp.concatenate([left] + [shift(left, s, 0) for s in (1, -1, 2)], axis=1)
    below, above = shift(line, 0, 1), shift(line, 0, -1)
    lefts = [line, below, above, shift(below[:HALF], 0, 1), shift(above[HALF:], 0, -1)]
    lefts = lefts + [swap(g) for g in lefts]

    nears = [near[0]] + [shift(piece, *step) for piece, step in zip(near[1:], steps[1:])]
    nears.append(swap(jnp.stack([piece[1] for piece in nears])))

    left, partial = near_product(lefts, nears)
    inflated, totals = far_product(c_pattern, left, partial, fars)
    gathered = lax.all_to_all(totals, "row", split_axis=0, concat_axis=0, tiled=True)
    return rescale(gathered, inflated)


def solution(mesh):
    return jax.shard_map(
        shards,
        mesh=mesh,
        in_specs=(
            P("row", "col"),
            P("col", None),
            P("row", "col"),
            P("col", None),
            P("row", "col"),
        ),
        out_specs=P("row", "col"),
        check_vma=False,
    )
```

```python
import functools

import jax
import jax.numpy as jnp
from jax import lax
from jax.experimental import pallas as pl
from jax.experimental.pallas import tpu as pltpu
from jax.sharding import PartitionSpec as P

BLOCK = 128
XS, YS, CORES = 4, 4, 2
COLS = XS * YS * CORES
ROWS = 8
EPS = 1e-06
F32 = jnp.float32
BF16 = jnp.bfloat16

OFFSETS = (0, -1, 1, 2)
NEAR = ((0, 0), (0, 1), (0, 2), (1, 0), (2, 0))
FAR = tuple((d, e) for d in range(4) for e in range(4) if (d, e) not in NEAR)


def flat(x, y, c):
    return ((x & (XS - 1)) * YS + (y & (YS - 1))) * CORES + c


def place(x, y, c, first, second):
    if isinstance(c, int):
        return flat(x + first, y + second, c) if c == 0 else flat(x + second, y + first, c)
    dx = jnp.where(c == 0, first, second)
    dy = jnp.where(c == 0, second, first)
    return flat(x + dx, y + dy, c)


def shift(value, first, second):
    pairs = []
    for x in range(XS):
        for y in range(YS):
            for c in range(CORES):
                pairs.append((flat(x, y, c), place(x, y, c, first, second)))
    return lax.ppermute(value, "col", pairs)


def swap(value):
    return lax.ppermute(value, "col", [(i, i ^ 1) for i in range(COLS)])


def smem():
    return pl.BlockSpec(memory_space=pltpu.SMEM)


def vmem():
    return pl.BlockSpec(memory_space=pltpu.VMEM)


def any_space():
    return pl.BlockSpec(memory_space=pl.ANY)


def params():
    return pltpu.CompilerParams(vmem_limit_bytes=56 * 1024 * 1024)


def held(value):
    return pltpu.with_memory_space_constraint(value, pltpu.VMEM)


def outside(value):
    return pltpu.with_memory_space_constraint(value, pltpu.HBM)


def limit(size):
    return pltpu.CompilerParams(vmem_limit_bytes=size << 20)


def mask_left_kernel(pattern_ref, a_ref, o_ref):
    for i in range(a_ref.shape[0] // BLOCK):
        rows = slice(i * BLOCK, (i + 1) * BLOCK)
        block = a_ref[rows, :]
        o_ref[rows, :] = jnp.where(pattern_ref[i, 0] != 0, block, jnp.zeros_like(block))


def mask_left(a, pattern):
    return pl.pallas_call(
        mask_left_kernel,
        out_shape=jax.ShapeDtypeStruct(a.shape, a.dtype),
        in_specs=[smem(), vmem()],
        out_specs=vmem(),
        compiler_params=params(),
        cost_estimate=pl.CostEstimate(flops=a.size, bytes_accessed=4 * a.size, transcendentals=0),
    )(pattern, a)


def spread_kernel(row_ref, pattern_ref, b_ref, o_ref, held, sems):
    row = row_ref[0]
    count = o_ref.shape[0]

    def copy(j):
        columns = pl.ds(pl.multiple_of((j * ROWS + row) * BLOCK, BLOCK), BLOCK)
        return pltpu.make_async_copy(b_ref.at[:, columns], held.at[j], sems.at[j])

    for j in range(count):
        copy(j).start()
    for j in range(count):
        copy(j).wait()
        block = held[j]
        o_ref[j] = jnp.where(pattern_ref[0, j * ROWS + row] != 0, block, jnp.zeros_like(block))


def spread(b, pattern, row):
    shape = (COLS, b.shape[0], BLOCK)
    return pl.pallas_call(
        spread_kernel,
        out_shape=jax.ShapeDtypeStruct(shape, b.dtype),
        in_specs=[smem(), smem(), any_space()],
        out_specs=vmem(),
        scratch_shapes=[pltpu.VMEM(shape, b.dtype), pltpu.SemaphoreType.DMA((COLS,))],
        compiler_params=params(),
        cost_estimate=pl.CostEstimate(flops=1 << 20, bytes_accessed=1 << 21, transcendentals=0),
    )(row, pattern, b)


def pieces_kernel(where_ref, pattern_ref, b_ref, *rest):
    count = len(NEAR)
    outs, held, sems = rest[:count], rest[count], rest[count + 1]
    width = outs[0].shape[2]
    blocks = width // BLOCK

    def copy(k):
        columns = pl.ds(pl.multiple_of(where_ref[k] * width, width), width)
        return pltpu.make_async_copy(b_ref.at[:, columns], held.at[k], sems.at[k])

    for k in range(2 * count):
        copy(k).start()
    for k in range(2 * count):
        copy(k).wait()
        for i in range(blocks):
            columns = slice(i * BLOCK, (i + 1) * BLOCK)
            block = held[k, :, columns]
            keep = pattern_ref[0, where_ref[k] * blocks + i] != 0
            outs[k // 2][k % 2, :, columns] = jnp.where(keep, block, jnp.zeros_like(block))


def pieces(b, pattern, where):
    width, count = b.shape[1] // COLS, len(NEAR)
    shape = (2, b.shape[0], width)
    return pl.pallas_call(
        pieces_kernel,
        out_shape=[jax.ShapeDtypeStruct(shape, b.dtype)] * count,
        in_specs=[smem(), smem(), any_space()],
        out_specs=[vmem()] * count,
        scratch_shapes=[
            pltpu.VMEM((2 * count, b.shape[0], width), b.dtype),
            pltpu.SemaphoreType.DMA((2 * count,)),
        ],
        compiler_params=params(),
        cost_estimate=pl.CostEstimate(flops=4 << 20, bytes_accessed=8 << 20, transcendentals=0),
    )(where, pattern, b)


def select_kernel(index_ref, r_ref, o_ref):
    for j in range(o_ref.shape[0]):
        o_ref[j] = r_ref[index_ref[j]]


def select(received, index):
    count = index.shape[0]
    return pl.pallas_call(
        select_kernel,
        out_shape=jax.ShapeDtypeStruct((count,) + received.shape[1:], received.dtype),
        in_specs=[smem(), vmem()],
        out_specs=vmem(),
        compiler_params=params(),
        cost_estimate=pl.CostEstimate(flops=0, bytes_accessed=2 << 20, transcendentals=0),
    )(index, held(received))


CHUNK = 384
HALF = 768


def runs(o, d):
    found = []
    for e in range(4):
        if (d, e) in FAR:
            spot = o * len(FAR) + FAR.index((d, e))
        else:
            spot = 2 * len(FAR) + o * len(NEAR) + NEAR.index((d, e))
        if found and found[-1][2] + found[-1][1] == spot:
            found[-1][1] += 1
        else:
            found.append([e, 1, spot])
    return found


def pairs_of(fars, far, sems):
    sources = 2 * len(FAR)
    return [
        pltpu.make_async_copy(
            fars.at[pl.ds(n * sources, sources)],
            far.at[n // 2, :, :, pl.ds(n % 2 * BLOCK, BLOCK)],
            sems.at[n],
        )
        for n in range(ROWS)
    ]


def first_kernel(*refs):
    refs = list(refs)
    lefts = [refs.pop(0) for _ in range(10)]
    nears = [refs.pop(0) for _ in range(len(NEAR) + 1)]
    left_out, o_ref, left, piece, near, out, nsem, lsem, osem = refs
    rows, count, depth = o_ref.shape[0], len(NEAR), 2 * len(FAR) * BLOCK

    whole = [pltpu.make_async_copy(nears[k].at[0], near.at[k], nsem.at[k]) for k in range(count)]
    whole.append(pltpu.make_async_copy(nears[count], near.at[pl.ds(count, count)], nsem.at[count]))
    parts = []
    for i in range(rows // CHUNK):
        start = i * CHUNK
        part = []
        for k in range(8):
            o, d = k // 4, k % 4
            if d < 3:
                source = lefts[o * 5 + d].at[pl.ds(start, CHUNK), :]
            else:
                source = lefts[o * 5 + 3 + start // HALF].at[pl.ds(start % HALF, CHUNK), :]
            part.append(pltpu.make_async_copy(source, piece.at[i % 2, k], lsem.at[i * 8 + k]))
        parts.append(part)
    for group in (parts[0], whole, parts[1]):
        for copy in group:
            copy.start()
    outs = []
    for i, part in enumerate(parts):
        here, slot = pl.ds(i * CHUNK, CHUNK), i % 2
        for copy in part:
            copy.wait()
        if i >= 2:
            for copy in outs[i - 2]:
                copy.wait()
        for k in range(8):
            for block, width, spot in runs(k // 4, k % 4):
                lanes = slice(block * BLOCK, (block + width) * BLOCK)
                target = slice(spot * BLOCK, (spot + width) * BLOCK)
                left[slot, :, target] = piece[slot, k, :, lanes]
        if i + 2 < len(parts):
            for copy in parts[i + 2]:
                copy.start()
        outs.append([
            pltpu.make_async_copy(left.at[slot, :, pl.ds(0, depth)], left_out.at[here, :], osem.at[2 * i]),
            pltpu.make_async_copy(out.at[slot], o_ref.at[here, :], osem.at[2 * i + 1]),
        ])
        outs[i][0].start()
        if i == 0:
            for copy in whole:
                copy.wait()
        out[slot] = jnp.dot(
            left[slot, :, depth:],
            near[...].reshape(2 * count * BLOCK, ROWS * BLOCK),
            preferred_element_type=F32,
        )
        outs[i][1].start()
    for pair in outs[-2:]:
        for copy in pair:
            copy.wait()


def second_kernel(cpat_ref, left_in, sum_in, fars, o_ref, t_ref, left, partial, far, fsem, lsem):
    rows, depth = o_ref.shape[0], 2 * len(FAR) * BLOCK
    blocks = pairs_of(fars, far, fsem)
    parts = []
    for i in range(rows // CHUNK):
        here = pl.ds(i * CHUNK, CHUNK)
        parts.append([
            pltpu.make_async_copy(left_in.at[here, :], left.at[here, :], lsem.at[2 * i]),
            pltpu.make_async_copy(sum_in.at[here, :], partial.at[here, :], lsem.at[2 * i + 1]),
        ])
    for group in (blocks[:2], parts[0], blocks[2:], *parts[1:]):
        for copy in group:
            copy.start()
    sums = [jnp.zeros((1, BLOCK), F32) for _ in range(ROWS)]
    for i, part in enumerate(parts):
        start, stop = i * CHUNK, (i + 1) * CHUNK
        for copy in part:
            copy.wait()
        for pair in range(ROWS // 2):
            if i == 0:
                for copy in blocks[2 * pair:2 * pair + 2]:
                    copy.wait()
            product = jnp.dot(
                left[start:stop, :], far[pair].reshape(depth, 2 * BLOCK), preferred_element_type=F32
            )
            for n in range(2):
                lanes = slice(n * BLOCK, (n + 1) * BLOCK)
                column = 2 * pair + n
                target = slice(column * BLOCK, (column + 1) * BLOCK)
                for j in range(CHUNK // BLOCK):
                    keep = cpat_ref[start // BLOCK + j, column] != 0
                    place = slice(start + j * BLOCK, start + (j + 1) * BLOCK)
                    block = product[j * BLOCK:(j + 1) * BLOCK, lanes] + partial[place, target]
                    block = jnp.where(keep, block * block, jnp.zeros_like(block))
                    o_ref[place, target] = block
                    sums[column] = sums[column] + jnp.sum(block, axis=0, keepdims=True)
    for r in range(ROWS):
        for n in range(ROWS):
            t_ref[r, n:n + 1, :] = sums[n]


def cost(rows, sources, data):
    return pl.CostEstimate(
        flops=2 * rows * sources * BLOCK * ROWS * BLOCK, bytes_accessed=data << 20, transcendentals=0
    )


def first_product(lefts, nears):
    rows, sources = 2 * HALF, 2 * len(FAR)
    return pl.pallas_call(
        first_kernel,
        out_shape=[pltpu.HBM((rows, sources * BLOCK), BF16), pltpu.HBM((rows, ROWS * BLOCK), F32)],
        in_specs=[any_space()] * (len(lefts) + len(nears)),
        out_specs=[any_space()] * 2,
        scratch_shapes=[
            pltpu.VMEM((2, CHUNK, COLS * BLOCK), BF16),
            pltpu.VMEM((2, 8, CHUNK, 512), BF16),
            pltpu.VMEM((2 * len(NEAR), BLOCK, ROWS * BLOCK), BF16),
            pltpu.VMEM((2, CHUNK, ROWS * BLOCK), F32),
            pltpu.SemaphoreType.DMA((len(nears),)),
            pltpu.SemaphoreType.DMA((32,)),
            pltpu.SemaphoreType.DMA((8,)),
        ],
        compiler_params=limit(24),
        cost_estimate=cost(rows, 2 * len(NEAR), 32),
    )(*lefts, *[outside(array) for array in nears])


def second_product(cpat, left, partial, fars):
    rows, depth = left.shape
    return pl.pallas_call(
        second_kernel,
        out_shape=[
            pltpu.VMEM((rows, ROWS * BLOCK), F32),
            jax.ShapeDtypeStruct((ROWS, ROWS, BLOCK), F32),
        ],
        in_specs=[smem()] + [any_space()] * 3,
        out_specs=[vmem()] * 2,
        scratch_shapes=[
            pltpu.VMEM((rows, depth), BF16),
            pltpu.VMEM((rows, ROWS * BLOCK), F32),
            pltpu.VMEM((ROWS // 2, 2 * len(FAR), BLOCK, 2 * BLOCK), BF16),
            pltpu.SemaphoreType.DMA((ROWS,)),
            pltpu.SemaphoreType.DMA((8,)),
        ],
        compiler_params=limit(32),
        cost_estimate=cost(rows, 2 * len(FAR), 24),
    )(cpat, outside(left), outside(partial), outside(fars))


def rescale_kernel(count, t_ref, i_ref, o_ref):
    total = t_ref[0]
    for r in range(1, ROWS):
        total = total + t_ref[r]
    scale = count / (total + EPS)
    rows = pl.ds(pl.program_id(0) * o_ref.shape[0], o_ref.shape[0])
    for n in range(ROWS):
        lanes = slice(n * BLOCK, (n + 1) * BLOCK)
        o_ref[:, lanes] = (i_ref[rows, lanes] * scale[n:n + 1, :]).astype(BF16)


def rescale(totals, inflated):
    rows, columns = inflated.shape
    tile = 256
    return pl.pallas_call(
        functools.partial(rescale_kernel, float(rows * ROWS)),
        out_shape=jax.ShapeDtypeStruct((rows, columns), BF16),
        grid=(rows // tile,),
        in_specs=[pl.BlockSpec(totals.shape, lambda i: (0, 0, 0)), vmem()],
        out_specs=pl.BlockSpec((tile, columns), lambda i: (i, 0)),
        compiler_params=limit(16),
        cost_estimate=pl.CostEstimate(flops=rows * 2048, bytes_accessed=4 << 20, transcendentals=0),
    )(totals, held(inflated))


def shards(a_values, b_values, a_pattern, b_pattern, c_pattern):
    col = lax.axis_index("col").astype(jnp.int32)
    row = lax.axis_index("row").astype(jnp.int32)
    x, y, c = col >> 3, (col >> 1) & (YS - 1), col & (CORES - 1)

    sent = spread(b_values, b_pattern, row[None])
    received = lax.all_to_all(sent, "col", split_axis=0, concat_axis=0, tiled=True)

    left = mask_left(a_values, a_pattern)
    where = []
    steps = ((0, 0), (1, 0), (-1, 0), (0, 1), (0, -1))
    for first, second in steps:
        there = place(x, y, c, first, second)
        where += [there, there ^ 1]
    near = pieces(b_values, b_pattern, jnp.stack(where))
    index = []
    for core in (c, 1 - c):
        for d, e in FAR:
            index.append(place(x, y, core, OFFSETS[e], OFFSETS[d]))
    received, left, near = lax.optimization_barrier((received, left, near))
    own = select(received, jnp.stack(index))
    left, near, _ = lax.optimization_barrier((left, near, own))

    fars = lax.all_gather(own, "row", axis=0, tiled=True)

    line = jnp.concatenate([left] + [shift(left, s, 0) for s in (1, -1, 2)], axis=1)
    below, above = shift(line, 0, 1), shift(line, 0, -1)
    lefts = [line, below, above, shift(below[:HALF], 0, 1), shift(above[HALF:], 0, -1)]
    lefts = lefts + [swap(g) for g in lefts]

    nears = [near[0]] + [shift(piece, *step) for piece, step in zip(near[1:], steps[1:])]
    nears.append(swap(jnp.stack([piece[1] for piece in nears])))

    left, partial = first_product(lefts, nears)
    inflated, totals = second_product(c_pattern, left, partial, fars)
    gathered = lax.all_to_all(totals, "row", split_axis=0, concat_axis=0, tiled=True)
    return rescale(gathered, inflated)


def solution(mesh):
    return jax.shard_map(
        shards,
        mesh=mesh,
        in_specs=(
            P("row", "col"),
            P("col", None),
            P("row", "col"),
            P("col", None),
            P("row", "col"),
        ),
        out_specs=P("row", "col"),
        check_vma=False,
    )
```

```python
import functools

import jax
import jax.numpy as jnp
from jax import lax
from jax.experimental import pallas as pl
from jax.experimental.pallas import tpu as pltpu
from jax.sharding import PartitionSpec as P

BLOCK = 128
XS, YS, CORES = 4, 4, 2
COLS = XS * YS * CORES
ROWS = 8
EPS = 1e-06
F32 = jnp.float32
BF16 = jnp.bfloat16

OFFSETS = (0, -1, 1, 2)
NEAR = ((0, 0), (0, 1), (0, 2), (1, 0), (2, 0))
FAR = tuple((d, e) for d in range(4) for e in range(4) if (d, e) not in NEAR)


def flat(x, y, c):
    return ((x & (XS - 1)) * YS + (y & (YS - 1))) * CORES + c


def place(x, y, c, first, second):
    if isinstance(c, int):
        return flat(x + first, y + second, c) if c == 0 else flat(x + second, y + first, c)
    dx = jnp.where(c == 0, first, second)
    dy = jnp.where(c == 0, second, first)
    return flat(x + dx, y + dy, c)


def shift(value, first, second):
    pairs = []
    for x in range(XS):
        for y in range(YS):
            for c in range(CORES):
                pairs.append((flat(x, y, c), place(x, y, c, first, second)))
    return lax.ppermute(value, "col", pairs)


def swap(value):
    return lax.ppermute(value, "col", [(i, i ^ 1) for i in range(COLS)])


def smem():
    return pl.BlockSpec(memory_space=pltpu.SMEM)


def vmem():
    return pl.BlockSpec(memory_space=pltpu.VMEM)


def any_space():
    return pl.BlockSpec(memory_space=pl.ANY)


def params():
    return pltpu.CompilerParams(vmem_limit_bytes=56 * 1024 * 1024)


def held(value):
    return pltpu.with_memory_space_constraint(value, pltpu.VMEM)


def outside(value):
    return pltpu.with_memory_space_constraint(value, pltpu.HBM)


def limit(size):
    return pltpu.CompilerParams(vmem_limit_bytes=size << 20)


def mask_left_kernel(pattern_ref, a_ref, o_ref):
    for i in range(a_ref.shape[0] // BLOCK):
        rows = slice(i * BLOCK, (i + 1) * BLOCK)
        block = a_ref[rows, :]
        o_ref[rows, :] = jnp.where(pattern_ref[i, 0] != 0, block, jnp.zeros_like(block))


def mask_left(a, pattern):
    return pl.pallas_call(
        mask_left_kernel,
        out_shape=jax.ShapeDtypeStruct(a.shape, a.dtype),
        in_specs=[smem(), vmem()],
        out_specs=vmem(),
        compiler_params=params(),
        cost_estimate=pl.CostEstimate(flops=a.size, bytes_accessed=4 * a.size, transcendentals=0),
    )(pattern, a)


def spread_kernel(row_ref, pattern_ref, b_ref, o_ref, held, sems):
    row = row_ref[0]
    count = o_ref.shape[0]

    def copy(j):
        columns = pl.ds(pl.multiple_of((j * ROWS + row) * BLOCK, BLOCK), BLOCK)
        return pltpu.make_async_copy(b_ref.at[:, columns], held.at[j], sems.at[j])

    for j in range(count):
        copy(j).start()
    for j in range(count):
        copy(j).wait()
        block = held[j]
        o_ref[j] = jnp.where(pattern_ref[0, j * ROWS + row] != 0, block, jnp.zeros_like(block))


def spread(b, pattern, row):
    shape = (COLS, b.shape[0], BLOCK)
    return pl.pallas_call(
        spread_kernel,
        out_shape=pltpu.VMEM(shape, b.dtype),
        in_specs=[smem(), smem(), any_space()],
        out_specs=vmem(),
        scratch_shapes=[pltpu.VMEM(shape, b.dtype), pltpu.SemaphoreType.DMA((COLS,))],
        compiler_params=params(),
        cost_estimate=pl.CostEstimate(flops=1 << 20, bytes_accessed=1 << 21, transcendentals=0),
    )(row, pattern, b)


def pieces_kernel(where_ref, pattern_ref, b_ref, *rest):
    count = len(NEAR)
    outs, held, sems = rest[:count], rest[count], rest[count + 1]
    width = outs[0].shape[2]
    blocks = width // BLOCK

    def copy(k):
        columns = pl.ds(pl.multiple_of(where_ref[k] * width, width), width)
        return pltpu.make_async_copy(b_ref.at[:, columns], held.at[k], sems.at[k])

    for k in range(2 * count):
        copy(k).start()
    for k in range(2 * count):
        copy(k).wait()
        for i in range(blocks):
            columns = slice(i * BLOCK, (i + 1) * BLOCK)
            block = held[k, :, columns]
            keep = pattern_ref[0, where_ref[k] * blocks + i] != 0
            outs[k // 2][k % 2, :, columns] = jnp.where(keep, block, jnp.zeros_like(block))


def pieces(b, pattern, where):
    width, count = b.shape[1] // COLS, len(NEAR)
    shape = (2, b.shape[0], width)
    return pl.pallas_call(
        pieces_kernel,
        out_shape=[jax.ShapeDtypeStruct(shape, b.dtype)] * count,
        in_specs=[smem(), smem(), any_space()],
        out_specs=[vmem()] * count,
        scratch_shapes=[
            pltpu.VMEM((2 * count, b.shape[0], width), b.dtype),
            pltpu.SemaphoreType.DMA((2 * count,)),
        ],
        compiler_params=params(),
        cost_estimate=pl.CostEstimate(flops=4 << 20, bytes_accessed=8 << 20, transcendentals=0),
    )(where, pattern, b)


def select_kernel(index_ref, r_ref, o_ref):
    for j in range(o_ref.shape[0]):
        o_ref[j] = r_ref[index_ref[j]]


def select(received, index):
    count = index.shape[0]
    return pl.pallas_call(
        select_kernel,
        out_shape=jax.ShapeDtypeStruct((count,) + received.shape[1:], received.dtype),
        in_specs=[smem(), vmem()],
        out_specs=vmem(),
        compiler_params=params(),
        cost_estimate=pl.CostEstimate(flops=0, bytes_accessed=2 << 20, transcendentals=0),
    )(index, held(received))


CHUNK = 384
CHUNKS = ((0, 768), (768, 768))
WIDE = 4
HALF = 768


def runs(o, d):
    found = []
    for e in range(4):
        if (d, e) in FAR:
            spot = o * len(FAR) + FAR.index((d, e))
        else:
            spot = 2 * len(FAR) + o * len(NEAR) + NEAR.index((d, e))
        if found and found[-1][2] + found[-1][1] == spot:
            found[-1][1] += 1
        else:
            found.append([e, 1, spot])
    return found


def pairs_of(fars, far, sems):
    sources = 2 * len(FAR)
    return [
        pltpu.make_async_copy(
            fars.at[pl.ds(n * sources, sources)],
            far.at[n // WIDE, :, :, pl.ds(n % WIDE * BLOCK, BLOCK)],
            sems.at[n],
        )
        for n in range(ROWS)
    ]


def first_kernel(*refs):
    refs = list(refs)
    lefts = [refs.pop(0) for _ in range(10)]
    nears = [refs.pop(0) for _ in range(len(NEAR) + 1)]
    left_out, o_ref, left, piece, near, out, nsem, lsem, osem = refs
    rows, count, depth = o_ref.shape[0], len(NEAR), 2 * len(FAR) * BLOCK

    whole = [pltpu.make_async_copy(nears[k].at[0], near.at[k], nsem.at[k]) for k in range(count)]
    whole.append(pltpu.make_async_copy(nears[count], near.at[pl.ds(count, count)], nsem.at[count]))
    parts = []
    for i in range(rows // CHUNK):
        start = i * CHUNK
        part = []
        for k in range(8):
            o, d = k // 4, k % 4
            if d < 3:
                source = lefts[o * 5 + d].at[pl.ds(start, CHUNK), :]
            else:
                source = lefts[o * 5 + 3 + start // HALF].at[pl.ds(start % HALF, CHUNK), :]
            part.append(pltpu.make_async_copy(source, piece.at[i % 2, k], lsem.at[i * 8 + k]))
        parts.append(part)
    for group in (parts[0], whole, parts[1]):
        for copy in group:
            copy.start()
    outs = []
    for i, part in enumerate(parts):
        here, slot = pl.ds(i * CHUNK, CHUNK), i % 2
        for copy in part:
            copy.wait()
        if i >= 2:
            for copy in outs[i - 2]:
                copy.wait()
        for k in range(8):
            for block, width, spot in runs(k // 4, k % 4):
                lanes = slice(block * BLOCK, (block + width) * BLOCK)
                target = slice(spot * BLOCK, (spot + width) * BLOCK)
                left[slot, :, target] = piece[slot, k, :, lanes]
        if i + 2 < len(parts):
            for copy in parts[i + 2]:
                copy.start()
        outs.append([
            pltpu.make_async_copy(left.at[slot, :, pl.ds(0, depth)], left_out.at[here, :], osem.at[2 * i]),
            pltpu.make_async_copy(out.at[slot], o_ref.at[here, :], osem.at[2 * i + 1]),
        ])
        outs[i][0].start()
        if i == 0:
            for copy in whole:
                copy.wait()
        out[slot] = jnp.dot(
            left[slot, :, depth:],
            near[...].reshape(2 * count * BLOCK, ROWS * BLOCK),
            preferred_element_type=F32,
        )
        outs[i][1].start()
    for pair in outs[-2:]:
        for copy in pair:
            copy.wait()


def second_kernel(cpat_ref, left_in, sum_in, fars, o_ref, t_ref, left, partial, far, fsem, lsem):
    depth = 2 * len(FAR) * BLOCK
    blocks = pairs_of(fars, far, fsem)
    parts = []
    for i, (start, size) in enumerate(CHUNKS):
        here = pl.ds(start, size)
        parts.append([
            pltpu.make_async_copy(left_in.at[here, :], left.at[here, :], lsem.at[2 * i]),
            pltpu.make_async_copy(sum_in.at[here, :], partial.at[here, :], lsem.at[2 * i + 1]),
        ])
    for group in (blocks[:WIDE], parts[0], blocks[WIDE:], *parts[1:]):
        for copy in group:
            copy.start()
    sums = [jnp.zeros((1, BLOCK), F32) for _ in range(ROWS)]
    for i, part in enumerate(parts):
        start, size = CHUNKS[i]
        for copy in part:
            copy.wait()
        for group in range(ROWS // WIDE):
            if i == 0:
                for copy in blocks[WIDE * group:WIDE * group + WIDE]:
                    copy.wait()
            product = jnp.dot(
                left[start:start + size, :],
                far[group].reshape(depth, WIDE * BLOCK),
                preferred_element_type=F32,
            )
            for n in range(WIDE):
                lanes = slice(n * BLOCK, (n + 1) * BLOCK)
                column = WIDE * group + n
                target = slice(column * BLOCK, (column + 1) * BLOCK)
                for j in range(size // BLOCK):
                    keep = cpat_ref[start // BLOCK + j, column] != 0
                    place = slice(start + j * BLOCK, start + (j + 1) * BLOCK)
                    block = product[j * BLOCK:(j + 1) * BLOCK, lanes] + partial[place, target]
                    block = jnp.where(keep, block * block, jnp.zeros_like(block))
                    o_ref[place, target] = block
                    sums[column] = sums[column] + jnp.sum(block, axis=0, keepdims=True)
    for r in range(ROWS):
        for n in range(ROWS):
            t_ref[r, n:n + 1, :] = sums[n]


def cost(rows, sources, data):
    return pl.CostEstimate(
        flops=2 * rows * sources * BLOCK * ROWS * BLOCK, bytes_accessed=data << 20, transcendentals=0
    )


def first_product(lefts, nears):
    rows, sources = 2 * HALF, 2 * len(FAR)
    return pl.pallas_call(
        first_kernel,
        out_shape=[pltpu.HBM((rows, sources * BLOCK), BF16), pltpu.HBM((rows, ROWS * BLOCK), F32)],
        in_specs=[any_space()] * (len(lefts) + len(nears)),
        out_specs=[any_space()] * 2,
        scratch_shapes=[
            pltpu.VMEM((2, CHUNK, COLS * BLOCK), BF16),
            pltpu.VMEM((2, 8, CHUNK, 512), BF16),
            pltpu.VMEM((2 * len(NEAR), BLOCK, ROWS * BLOCK), BF16),
            pltpu.VMEM((2, CHUNK, ROWS * BLOCK), F32),
            pltpu.SemaphoreType.DMA((len(nears),)),
            pltpu.SemaphoreType.DMA((32,)),
            pltpu.SemaphoreType.DMA((8,)),
        ],
        compiler_params=limit(24),
        cost_estimate=cost(rows, 2 * len(NEAR), 32),
    )(*lefts, *[outside(array) for array in nears])


def second_product(cpat, left, partial, fars):
    rows, depth = left.shape
    return pl.pallas_call(
        second_kernel,
        out_shape=[
            pltpu.VMEM((rows, ROWS * BLOCK), F32),
            jax.ShapeDtypeStruct((ROWS, ROWS, BLOCK), F32),
        ],
        in_specs=[smem()] + [any_space()] * 3,
        out_specs=[vmem()] * 2,
        scratch_shapes=[
            pltpu.VMEM((rows, depth), BF16),
            pltpu.VMEM((rows, ROWS * BLOCK), F32),
            pltpu.VMEM((ROWS // WIDE, 2 * len(FAR), BLOCK, WIDE * BLOCK), BF16),
            pltpu.SemaphoreType.DMA((ROWS,)),
            pltpu.SemaphoreType.DMA((8,)),
        ],
        compiler_params=limit(32),
        cost_estimate=cost(rows, 2 * len(FAR), 24),
    )(cpat, outside(left), outside(partial), outside(fars))


def rescale_kernel(count, t_ref, i_ref, o_ref):
    total = t_ref[0]
    for r in range(1, ROWS):
        total = total + t_ref[r]
    scale = count / (total + EPS)
    rows = pl.ds(pl.program_id(0) * o_ref.shape[0], o_ref.shape[0])
    for n in range(ROWS):
        lanes = slice(n * BLOCK, (n + 1) * BLOCK)
        o_ref[:, lanes] = (i_ref[rows, lanes] * scale[n:n + 1, :]).astype(BF16)


def rescale(totals, inflated):
    rows, columns = inflated.shape
    tile = 512
    return pl.pallas_call(
        functools.partial(rescale_kernel, float(rows * ROWS)),
        out_shape=jax.ShapeDtypeStruct((rows, columns), BF16),
        grid=(rows // tile,),
        in_specs=[pl.BlockSpec(totals.shape, lambda i: (0, 0, 0)), vmem()],
        out_specs=pl.BlockSpec((tile, columns), lambda i: (i, 0)),
        compiler_params=limit(16),
        cost_estimate=pl.CostEstimate(flops=rows * 2048, bytes_accessed=4 << 20, transcendentals=0),
    )(totals, held(inflated))


def shards(a_values, b_values, a_pattern, b_pattern, c_pattern):
    col = lax.axis_index("col").astype(jnp.int32)
    row = lax.axis_index("row").astype(jnp.int32)
    x, y, c = col >> 3, (col >> 1) & (YS - 1), col & (CORES - 1)

    sent = spread(b_values, b_pattern, row[None])
    received = lax.all_to_all(sent, "col", split_axis=0, concat_axis=0, tiled=True)

    left = mask_left(a_values, a_pattern)
    where = []
    steps = ((0, 0), (1, 0), (-1, 0), (0, 1), (0, -1))
    for first, second in steps:
        there = place(x, y, c, first, second)
        where += [there, there ^ 1]
    near = pieces(b_values, b_pattern, jnp.stack(where))
    index = []
    for core in (c, 1 - c):
        for d, e in FAR:
            index.append(place(x, y, core, OFFSETS[e], OFFSETS[d]))
    received, left, near = lax.optimization_barrier((received, left, near))
    own = select(received, jnp.stack(index))
    left, near, _ = lax.optimization_barrier((left, near, own))

    fars = lax.all_gather(own, "row", axis=0, tiled=True)

    line = jnp.concatenate([left] + [shift(left, s, 0) for s in (1, -1, 2)], axis=1)
    below, above = shift(line, 0, 1), shift(line, 0, -1)
    lefts = [line, below, above, shift(below[:HALF], 0, 1), shift(above[HALF:], 0, -1)]
    lefts = lefts + [swap(g) for g in lefts]

    nears = [near[0]] + [shift(piece, *step) for piece, step in zip(near[1:], steps[1:])]
    nears.append(swap(jnp.stack([piece[1] for piece in nears])))

    left, partial = first_product(lefts, nears)
    inflated, totals = second_product(c_pattern, left, partial, fars)
    gathered = lax.all_to_all(totals, "row", split_axis=0, concat_axis=0, tiled=True)
    return rescale(gathered, inflated)


def solution(mesh):
    return jax.shard_map(
        shards,
        mesh=mesh,
        in_specs=(
            P("row", "col"),
            P("col", None),
            P("row", "col"),
            P("col", None),
            P("row", "col"),
        ),
        out_specs=P("row", "col"),
        check_vma=False,
    )
```

```python
import functools

import jax
import jax.numpy as jnp
from jax import lax
from jax.experimental import pallas as pl
from jax.experimental.pallas import tpu as pltpu
from jax.sharding import PartitionSpec as P

BLOCK = 128
XS, YS, CORES = 4, 4, 2
COLS = XS * YS * CORES
ROWS = 8
EPS = 1e-06
F32 = jnp.float32
BF16 = jnp.bfloat16

OFFSETS = (0, -1, 1, 2)
NEAR = ((0, 0), (0, 1), (0, 2), (1, 0), (2, 0))
FAR = tuple((d, e) for d in range(4) for e in range(4) if (d, e) not in NEAR)


def flat(x, y, c):
    return ((x & (XS - 1)) * YS + (y & (YS - 1))) * CORES + c


def place(x, y, c, first, second):
    if isinstance(c, int):
        return flat(x + first, y + second, c) if c == 0 else flat(x + second, y + first, c)
    dx = jnp.where(c == 0, first, second)
    dy = jnp.where(c == 0, second, first)
    return flat(x + dx, y + dy, c)


def shift(value, first, second):
    pairs = []
    for x in range(XS):
        for y in range(YS):
            for c in range(CORES):
                pairs.append((flat(x, y, c), place(x, y, c, first, second)))
    return lax.ppermute(value, "col", pairs)


def swap(value):
    return lax.ppermute(value, "col", [(i, i ^ 1) for i in range(COLS)])


def smem():
    return pl.BlockSpec(memory_space=pltpu.SMEM)


def vmem():
    return pl.BlockSpec(memory_space=pltpu.VMEM)


def any_space():
    return pl.BlockSpec(memory_space=pl.ANY)


def params():
    return pltpu.CompilerParams(vmem_limit_bytes=56 * 1024 * 1024)


def held(value):
    return pltpu.with_memory_space_constraint(value, pltpu.VMEM)


def outside(value):
    return pltpu.with_memory_space_constraint(value, pltpu.HBM)


def limit(size):
    return pltpu.CompilerParams(vmem_limit_bytes=size << 20)


def mask_left_kernel(pattern_ref, a_ref, o_ref):
    for i in range(a_ref.shape[0] // BLOCK):
        rows = slice(i * BLOCK, (i + 1) * BLOCK)
        block = a_ref[rows, :]
        o_ref[rows, :] = jnp.where(pattern_ref[i, 0] != 0, block, jnp.zeros_like(block))


def mask_left(a, pattern):
    return pl.pallas_call(
        mask_left_kernel,
        out_shape=jax.ShapeDtypeStruct(a.shape, a.dtype),
        in_specs=[smem(), vmem()],
        out_specs=vmem(),
        compiler_params=params(),
        cost_estimate=pl.CostEstimate(flops=a.size, bytes_accessed=4 * a.size, transcendentals=0),
    )(pattern, a)


def spread_kernel(row_ref, pattern_ref, b_ref, o_ref, held, sems):
    row = row_ref[0]
    count = o_ref.shape[0]

    def copy(j):
        columns = pl.ds(pl.multiple_of((j * ROWS + row) * BLOCK, BLOCK), BLOCK)
        return pltpu.make_async_copy(b_ref.at[:, columns], held.at[j], sems.at[j])

    for j in range(count):
        copy(j).start()
    for j in range(count):
        copy(j).wait()
        block = held[j]
        o_ref[j] = jnp.where(pattern_ref[0, j * ROWS + row] != 0, block, jnp.zeros_like(block))


def spread(b, pattern, row):
    shape = (COLS, b.shape[0], BLOCK)
    return pl.pallas_call(
        spread_kernel,
        out_shape=pltpu.VMEM(shape, b.dtype),
        in_specs=[smem(), smem(), any_space()],
        out_specs=vmem(),
        scratch_shapes=[pltpu.VMEM(shape, b.dtype), pltpu.SemaphoreType.DMA((COLS,))],
        compiler_params=params(),
        cost_estimate=pl.CostEstimate(flops=1 << 20, bytes_accessed=1 << 21, transcendentals=0),
    )(row, pattern, b)


def pieces_kernel(where_ref, pattern_ref, b_ref, *rest):
    count = len(NEAR)
    outs, held, sems = rest[:count], rest[count], rest[count + 1]
    width = outs[0].shape[2]
    blocks = width // BLOCK

    def copy(k):
        columns = pl.ds(pl.multiple_of(where_ref[k] * width, width), width)
        return pltpu.make_async_copy(b_ref.at[:, columns], held.at[k], sems.at[k])

    for k in range(2 * count):
        copy(k).start()
    for k in range(2 * count):
        copy(k).wait()
        for i in range(blocks):
            columns = slice(i * BLOCK, (i + 1) * BLOCK)
            block = held[k, :, columns]
            keep = pattern_ref[0, where_ref[k] * blocks + i] != 0
            outs[k // 2][k % 2, :, columns] = jnp.where(keep, block, jnp.zeros_like(block))


def pieces(b, pattern, where):
    width, count = b.shape[1] // COLS, len(NEAR)
    shape = (2, b.shape[0], width)
    return pl.pallas_call(
        pieces_kernel,
        out_shape=[jax.ShapeDtypeStruct(shape, b.dtype)] * count,
        in_specs=[smem(), smem(), any_space()],
        out_specs=[vmem()] * count,
        scratch_shapes=[
            pltpu.VMEM((2 * count, b.shape[0], width), b.dtype),
            pltpu.SemaphoreType.DMA((2 * count,)),
        ],
        compiler_params=params(),
        cost_estimate=pl.CostEstimate(flops=4 << 20, bytes_accessed=8 << 20, transcendentals=0),
    )(where, pattern, b)


def select_kernel(index_ref, r_ref, o_ref):
    for j in range(o_ref.shape[0]):
        o_ref[j] = r_ref[index_ref[j]]


def select(received, index):
    count = index.shape[0]
    return pl.pallas_call(
        select_kernel,
        out_shape=jax.ShapeDtypeStruct((count,) + received.shape[1:], received.dtype),
        in_specs=[smem(), vmem()],
        out_specs=vmem(),
        compiler_params=params(),
        cost_estimate=pl.CostEstimate(flops=0, bytes_accessed=2 << 20, transcendentals=0),
    )(index, held(received))


HALF = 768
CHUNK = 384
CHUNKS = ((0, HALF), (HALF, HALF))
WIDE = 4


EARLY = len(FAR) - 4


def runs(o, d):
    found = []
    for e in range(4):
        if (d, e) in FAR:
            spot = o * len(FAR) + FAR.index((d, e))
        else:
            spot = 2 * len(FAR) + o * len(NEAR) + NEAR.index((d, e))
        if found and found[-1][2] + found[-1][1] == spot:
            found[-1][1] += 1
        else:
            found.append([e, 1, spot])
    return found


def pairs_of(fars, far, sems):
    sources = 2 * len(FAR)
    return [
        pltpu.make_async_copy(
            fars.at[pl.ds(n * sources, sources)],
            far.at[n // WIDE, :, :, pl.ds(n % WIDE * BLOCK, BLOCK)],
            sems.at[n],
        )
        for n in range(ROWS)
    ]


def first_kernel(*refs):
    refs = list(refs)
    lefts = [refs.pop(0) for _ in range(6)]
    nears = [refs.pop(0) for _ in range(len(NEAR) + 1)]
    left_out, o_ref, left, piece, near, out, nsem, lsem, osem = refs
    rows, count, depth = o_ref.shape[0], len(NEAR), 2 * EARLY * BLOCK

    whole = [pltpu.make_async_copy(nears[k].at[0], near.at[k], nsem.at[k]) for k in range(count)]
    whole.append(pltpu.make_async_copy(nears[count], near.at[pl.ds(count, count)], nsem.at[count]))
    parts = []
    for i in range(rows // CHUNK):
        start = i * CHUNK
        part = []
        for k in range(6):
            source = lefts[k].at[pl.ds(start, CHUNK), :]
            part.append(pltpu.make_async_copy(source, piece.at[i % 2, k], lsem.at[i * 6 + k]))
        parts.append(part)
    for group in (parts[0], whole, parts[1]):
        for copy in group:
            copy.start()
    outs = []
    for i, part in enumerate(parts):
        here, slot = pl.ds(i * CHUNK, CHUNK), i % 2
        for copy in part:
            copy.wait()
        if i >= 2:
            for copy in outs[i - 2]:
                copy.wait()
        for k in range(6):
            for block, width, spot in runs(k // 3, k % 3):
                spot -= 4 * (spot // len(FAR)) if spot < 2 * len(FAR) else 8
                lanes = slice(block * BLOCK, (block + width) * BLOCK)
                target = slice(spot * BLOCK, (spot + width) * BLOCK)
                left[slot, :, target] = piece[slot, k, :, lanes]
        if i + 2 < len(parts):
            for copy in parts[i + 2]:
                copy.start()
        outs.append([
            pltpu.make_async_copy(left.at[slot, :, pl.ds(0, depth)], left_out.at[here, :], osem.at[2 * i]),
            pltpu.make_async_copy(out.at[slot], o_ref.at[here, :], osem.at[2 * i + 1]),
        ])
        outs[i][0].start()
        if i == 0:
            for copy in whole:
                copy.wait()
        out[slot] = jnp.dot(
            left[slot, :, depth:],
            near[...].reshape(2 * count * BLOCK, ROWS * BLOCK),
            preferred_element_type=F32,
        )
        outs[i][1].start()
    for pair in outs[-2:]:
        for copy in pair:
            copy.wait()


def second_kernel(cpat_ref, left_in, u0, l0, u1, l1, sum_in, fars, o_ref, t_ref, left, partial, far, fsem, lsem):
    depth = 2 * len(FAR) * BLOCK
    blocks = pairs_of(fars, far, fsem)
    parts = []
    for i, (start, size) in enumerate(CHUNKS):
        here = pl.ds(start, size)
        part = [pltpu.make_async_copy(sum_in.at[here, :], partial.at[here, :], lsem.at[5 * i])]
        for o, opposite in enumerate(((u0, l0), (u1, l1))):
            wide, place = EARLY * BLOCK, o * len(FAR) * BLOCK
            early = left_in.at[here, pl.ds(o * wide, wide)]
            part.append(pltpu.make_async_copy(early, left.at[here, pl.ds(place, wide)], lsem.at[5 * i + 1 + o]))
            target = left.at[here, pl.ds(place + wide, 4 * BLOCK)]
            part.append(pltpu.make_async_copy(opposite[i], target, lsem.at[5 * i + 3 + o]))
        parts.append(part)
    for group in (blocks[:WIDE], parts[0], blocks[WIDE:], *parts[1:]):
        for copy in group:
            copy.start()
    sums = [jnp.zeros((1, BLOCK), F32) for _ in range(ROWS)]
    for i, part in enumerate(parts):
        start, size = CHUNKS[i]
        for copy in part:
            copy.wait()
        for group in range(ROWS // WIDE):
            if i == 0:
                for copy in blocks[WIDE * group:WIDE * group + WIDE]:
                    copy.wait()
            product = jnp.dot(
                left[start:start + size, :],
                far[group].reshape(depth, WIDE * BLOCK),
                preferred_element_type=F32,
            )
            for n in range(WIDE):
                lanes = slice(n * BLOCK, (n + 1) * BLOCK)
                column = WIDE * group + n
                target = slice(column * BLOCK, (column + 1) * BLOCK)
                for j in range(size // BLOCK):
                    keep = cpat_ref[start // BLOCK + j, column] != 0
                    place = slice(start + j * BLOCK, start + (j + 1) * BLOCK)
                    block = product[j * BLOCK:(j + 1) * BLOCK, lanes] + partial[place, target]
                    block = jnp.where(keep, block * block, jnp.zeros_like(block))
                    o_ref[place, target] = block
                    sums[column] = sums[column] + jnp.sum(block, axis=0, keepdims=True)
    for r in range(ROWS):
        for n in range(ROWS):
            t_ref[r, n:n + 1, :] = sums[n]


def cost(rows, sources, data):
    return pl.CostEstimate(
        flops=2 * rows * sources * BLOCK * ROWS * BLOCK, bytes_accessed=data << 20, transcendentals=0
    )


def first_product(lefts, nears):
    rows, sources = 2 * HALF, 2 * EARLY
    return pl.pallas_call(
        first_kernel,
        out_shape=[pltpu.HBM((rows, sources * BLOCK), BF16), pltpu.HBM((rows, ROWS * BLOCK), F32)],
        in_specs=[any_space()] * (len(lefts) + len(nears)),
        out_specs=[any_space()] * 2,
        scratch_shapes=[
            pltpu.VMEM((2, CHUNK, (COLS - 8) * BLOCK), BF16),
            pltpu.VMEM((2, 6, CHUNK, 512), BF16),
            pltpu.VMEM((2 * len(NEAR), BLOCK, ROWS * BLOCK), BF16),
            pltpu.VMEM((2, CHUNK, ROWS * BLOCK), F32),
            pltpu.SemaphoreType.DMA((len(nears),)),
            pltpu.SemaphoreType.DMA((32,)),
            pltpu.SemaphoreType.DMA((8,)),
        ],
        compiler_params=limit(24),
        cost_estimate=cost(rows, 2 * len(NEAR), 32),
    )(*lefts, *[outside(array) for array in nears])


def second_product(cpat, left, opposite, partial, fars):
    rows, depth = 2 * HALF, 2 * len(FAR) * BLOCK
    return pl.pallas_call(
        second_kernel,
        out_shape=[
            pltpu.VMEM((rows, ROWS * BLOCK), F32),
            jax.ShapeDtypeStruct((ROWS, ROWS, BLOCK), F32),
        ],
        in_specs=[smem()] + [any_space()] * 7,
        out_specs=[vmem()] * 2,
        scratch_shapes=[
            pltpu.VMEM((rows, depth), BF16),
            pltpu.VMEM((rows, ROWS * BLOCK), F32),
            pltpu.VMEM((ROWS // WIDE, 2 * len(FAR), BLOCK, WIDE * BLOCK), BF16),
            pltpu.SemaphoreType.DMA((ROWS,)),
            pltpu.SemaphoreType.DMA((10,)),
        ],
        compiler_params=limit(32),
        cost_estimate=cost(rows, 2 * len(FAR), 24),
    )(cpat, outside(left), *opposite, outside(partial), outside(fars))


def rescale_kernel(count, t_ref, i_ref, o_ref):
    total = t_ref[0]
    for r in range(1, ROWS):
        total = total + t_ref[r]
    scale = count / (total + EPS)
    rows = pl.ds(pl.program_id(0) * o_ref.shape[0], o_ref.shape[0])
    for n in range(ROWS):
        lanes = slice(n * BLOCK, (n + 1) * BLOCK)
        o_ref[:, lanes] = (i_ref[rows, lanes] * scale[n:n + 1, :]).astype(BF16)


def rescale(totals, inflated):
    rows, columns = inflated.shape
    tile = 512
    return pl.pallas_call(
        functools.partial(rescale_kernel, float(rows * ROWS)),
        out_shape=jax.ShapeDtypeStruct((rows, columns), BF16),
        grid=(rows // tile,),
        in_specs=[pl.BlockSpec(totals.shape, lambda i: (0, 0, 0)), vmem()],
        out_specs=pl.BlockSpec((tile, columns), lambda i: (i, 0)),
        compiler_params=limit(16),
        cost_estimate=pl.CostEstimate(flops=rows * 2048, bytes_accessed=4 << 20, transcendentals=0),
    )(totals, held(inflated))


def shards(a_values, b_values, a_pattern, b_pattern, c_pattern):
    col = lax.axis_index("col").astype(jnp.int32)
    row = lax.axis_index("row").astype(jnp.int32)
    x, y, c = col >> 3, (col >> 1) & (YS - 1), col & (CORES - 1)

    sent = spread(b_values, b_pattern, row[None])
    received = lax.all_to_all(sent, "col", split_axis=0, concat_axis=0, tiled=True)

    left = mask_left(a_values, a_pattern)
    where = []
    steps = ((0, 0), (1, 0), (-1, 0), (0, 1), (0, -1))
    for first, second in steps:
        there = place(x, y, c, first, second)
        where += [there, there ^ 1]
    near = pieces(b_values, b_pattern, jnp.stack(where))
    index = []
    for core in (c, 1 - c):
        for d, e in FAR:
            index.append(place(x, y, core, OFFSETS[e], OFFSETS[d]))
    received, left, near = lax.optimization_barrier((received, left, near))
    own = select(received, jnp.stack(index))
    left, near, _ = lax.optimization_barrier((left, near, own))

    fars = lax.all_gather(own, "row", axis=0, tiled=True)

    line = jnp.concatenate([left] + [shift(left, s, 0) for s in (1, -1, 2)], axis=1)
    below, above = shift(line, 0, 1), shift(line, 0, -1)
    opposite = [shift(below[:HALF], 0, 1), shift(above[HALF:], 0, -1)]
    lefts = [line, below, above]
    lefts = lefts + [swap(g) for g in lefts]

    nears = [near[0]] + [shift(piece, *step) for piece, step in zip(near[1:], steps[1:])]
    nears.append(swap(jnp.stack([piece[1] for piece in nears])))

    left, partial = first_product(lefts, nears)
    opposite, partial = lax.optimization_barrier((opposite, partial))
    opposite = opposite + [swap(g) for g in opposite]
    inflated, totals = second_product(c_pattern, left, opposite, partial, fars)
    gathered = lax.all_to_all(totals, "row", split_axis=0, concat_axis=0, tiled=True)
    return rescale(gathered, inflated)


def solution(mesh):
    return jax.shard_map(
        shards,
        mesh=mesh,
        in_specs=(
            P("row", "col"),
            P("col", None),
            P("row", "col"),
            P("col", None),
            P("row", "col"),
        ),
        out_specs=P("row", "col"),
        check_vma=False,
    )
```

```python
import functools

import jax
import jax.numpy as jnp
from jax import lax
from jax.experimental import pallas as pl
from jax.experimental.pallas import tpu as pltpu
from jax.sharding import PartitionSpec as P

BLOCK = 128
XS, YS, CORES = 4, 4, 2
COLS = XS * YS * CORES
ROWS = 8
EPS = 1e-06
F32 = jnp.float32
BF16 = jnp.bfloat16

OFFSETS = (0, -1, 1, 2)
NEAR = ((0, 0), (0, 1), (0, 2), (1, 0), (2, 0))
FAR = tuple((d, e) for d in range(4) for e in range(4) if (d, e) not in NEAR)


def flat(x, y, c):
    return ((x & (XS - 1)) * YS + (y & (YS - 1))) * CORES + c


def place(x, y, c, first, second):
    if isinstance(c, int):
        return flat(x + first, y + second, c) if c == 0 else flat(x + second, y + first, c)
    dx = jnp.where(c == 0, first, second)
    dy = jnp.where(c == 0, second, first)
    return flat(x + dx, y + dy, c)


def shift(value, first, second):
    pairs = []
    for x in range(XS):
        for y in range(YS):
            for c in range(CORES):
                pairs.append((flat(x, y, c), place(x, y, c, first, second)))
    return lax.ppermute(value, "col", pairs)


def swap(value):
    return lax.ppermute(value, "col", [(i, i ^ 1) for i in range(COLS)])


def smem():
    return pl.BlockSpec(memory_space=pltpu.SMEM)


def vmem():
    return pl.BlockSpec(memory_space=pltpu.VMEM)


def any_space():
    return pl.BlockSpec(memory_space=pl.ANY)


def params():
    return pltpu.CompilerParams(vmem_limit_bytes=56 * 1024 * 1024)


def held(value):
    return pltpu.with_memory_space_constraint(value, pltpu.VMEM)


def outside(value):
    return pltpu.with_memory_space_constraint(value, pltpu.HBM)


def limit(size):
    return pltpu.CompilerParams(vmem_limit_bytes=size << 20)


def mask_left_kernel(pattern_ref, a_ref, o_ref):
    for i in range(a_ref.shape[0] // BLOCK):
        rows = slice(i * BLOCK, (i + 1) * BLOCK)
        block = a_ref[rows, :]
        o_ref[rows, :] = jnp.where(pattern_ref[i, 0] != 0, block, jnp.zeros_like(block))


def mask_left(a, pattern):
    return pl.pallas_call(
        mask_left_kernel,
        out_shape=jax.ShapeDtypeStruct(a.shape, a.dtype),
        in_specs=[smem(), vmem()],
        out_specs=vmem(),
        compiler_params=params(),
        cost_estimate=pl.CostEstimate(flops=a.size, bytes_accessed=4 * a.size, transcendentals=0),
    )(pattern, a)


def spread_kernel(row_ref, pattern_ref, b_ref, o_ref, held, sems):
    row = row_ref[0]
    count = o_ref.shape[0]

    def copy(j):
        columns = pl.ds(pl.multiple_of((j * ROWS + row) * BLOCK, BLOCK), BLOCK)
        return pltpu.make_async_copy(b_ref.at[:, columns], held.at[j], sems.at[j])

    for j in range(count):
        copy(j).start()
    for j in range(count):
        copy(j).wait()
        block = held[j]
        o_ref[j] = jnp.where(pattern_ref[0, j * ROWS + row] != 0, block, jnp.zeros_like(block))


def spread(b, pattern, row):
    shape = (COLS, b.shape[0], BLOCK)
    return pl.pallas_call(
        spread_kernel,
        out_shape=pltpu.VMEM(shape, b.dtype),
        in_specs=[smem(), smem(), any_space()],
        out_specs=vmem(),
        scratch_shapes=[pltpu.VMEM(shape, b.dtype), pltpu.SemaphoreType.DMA((COLS,))],
        compiler_params=params(),
        cost_estimate=pl.CostEstimate(flops=1 << 20, bytes_accessed=1 << 21, transcendentals=0),
    )(row, pattern, b)


def pieces_kernel(where_ref, pattern_ref, b_ref, *rest):
    count = len(NEAR)
    outs, held, sems = rest[:count], rest[count], rest[count + 1]
    width = outs[0].shape[2]
    blocks = width // BLOCK

    def copy(k):
        columns = pl.ds(pl.multiple_of(where_ref[k] * width, width), width)
        return pltpu.make_async_copy(b_ref.at[:, columns], held.at[k], sems.at[k])

    for k in range(2 * count):
        copy(k).start()
    for k in range(2 * count):
        copy(k).wait()
        for i in range(blocks):
            columns = slice(i * BLOCK, (i + 1) * BLOCK)
            block = held[k, :, columns]
            keep = pattern_ref[0, where_ref[k] * blocks + i] != 0
            outs[k // 2][k % 2, :, columns] = jnp.where(keep, block, jnp.zeros_like(block))


def pieces(b, pattern, where):
    width, count = b.shape[1] // COLS, len(NEAR)
    shape = (2, b.shape[0], width)
    return pl.pallas_call(
        pieces_kernel,
        out_shape=[jax.ShapeDtypeStruct(shape, b.dtype)] * count,
        in_specs=[smem(), smem(), any_space()],
        out_specs=[vmem()] * count,
        scratch_shapes=[
            pltpu.VMEM((2 * count, b.shape[0], width), b.dtype),
            pltpu.SemaphoreType.DMA((2 * count,)),
        ],
        compiler_params=params(),
        cost_estimate=pl.CostEstimate(flops=4 << 20, bytes_accessed=8 << 20, transcendentals=0),
    )(where, pattern, b)


def select_kernel(index_ref, r_ref, o_ref):
    for j in range(o_ref.shape[0]):
        o_ref[j] = r_ref[index_ref[j]]


def select(received, index):
    count = index.shape[0]
    return pl.pallas_call(
        select_kernel,
        out_shape=jax.ShapeDtypeStruct((count,) + received.shape[1:], received.dtype),
        in_specs=[smem(), vmem()],
        out_specs=vmem(),
        compiler_params=params(),
        cost_estimate=pl.CostEstimate(flops=0, bytes_accessed=2 << 20, transcendentals=0),
    )(index, held(received))


HALF = 768
CHUNK = 256
CHUNKS = ((0, HALF), (HALF, HALF))
WIDE = 4


EARLY = len(FAR) - 4


def runs(o, d):
    found = []
    for e in range(4):
        if (d, e) in FAR:
            spot = o * len(FAR) + FAR.index((d, e))
        else:
            spot = 2 * len(FAR) + o * len(NEAR) + NEAR.index((d, e))
        if found and found[-1][2] + found[-1][1] == spot:
            found[-1][1] += 1
        else:
            found.append([e, 1, spot])
    return found


def pairs_of(fars, far, sems):
    sources = 2 * len(FAR)
    return [
        pltpu.make_async_copy(
            fars.at[pl.ds(n * sources, sources)],
            far.at[n // WIDE, :, :, pl.ds(n % WIDE * BLOCK, BLOCK)],
            sems.at[n],
        )
        for n in range(ROWS)
    ]


def first_kernel(*refs):
    refs = list(refs)
    lefts = [refs.pop(0) for _ in range(6)]
    nears = [refs.pop(0) for _ in range(len(NEAR) + 1)]
    left_out, o_ref, left, piece, near, out, nsem, lsem, osem = refs
    rows, count, depth = o_ref.shape[0], len(NEAR), 2 * EARLY * BLOCK

    whole = [pltpu.make_async_copy(nears[k].at[0], near.at[k], nsem.at[k]) for k in range(count)]
    whole.append(pltpu.make_async_copy(nears[count], near.at[pl.ds(count, count)], nsem.at[count]))
    parts = []
    for i in range(rows // CHUNK):
        start = i * CHUNK
        part = []
        for k in range(6):
            source = lefts[k].at[pl.ds(start, CHUNK), :]
            part.append(pltpu.make_async_copy(source, piece.at[i % 2, k], lsem.at[i * 6 + k]))
        parts.append(part)
    for group in (parts[0], whole, parts[1]):
        for copy in group:
            copy.start()
    outs = []
    for i, part in enumerate(parts):
        here, slot = pl.ds(i * CHUNK, CHUNK), i % 2
        for copy in part:
            copy.wait()
        if i >= 2:
            for copy in outs[i - 2]:
                copy.wait()
        for k in range(6):
            for block, width, spot in runs(k // 3, k % 3):
                spot -= 4 * (spot // len(FAR)) if spot < 2 * len(FAR) else 8
                lanes = slice(block * BLOCK, (block + width) * BLOCK)
                target = slice(spot * BLOCK, (spot + width) * BLOCK)
                left[slot, :, target] = piece[slot, k, :, lanes]
        if i + 2 < len(parts):
            for copy in parts[i + 2]:
                copy.start()
        outs.append([
            pltpu.make_async_copy(left.at[slot, :, pl.ds(0, depth)], left_out.at[here, :], osem.at[2 * i]),
            pltpu.make_async_copy(out.at[slot], o_ref.at[here, :], osem.at[2 * i + 1]),
        ])
        outs[i][0].start()
        if i == 0:
            for copy in whole:
                copy.wait()
        out[slot] = jnp.dot(
            left[slot, :, depth:],
            near[...].reshape(2 * count * BLOCK, ROWS * BLOCK),
            preferred_element_type=F32,
        )
        outs[i][1].start()
    for pair in outs[-2:]:
        for copy in pair:
            copy.wait()


def second_kernel(cpat_ref, left_in, u0, l0, u1, l1, sum_in, fars, o_ref, t_ref, left, partial, far, fsem, lsem):
    depth = 2 * len(FAR) * BLOCK
    blocks = pairs_of(fars, far, fsem)
    parts = []
    for i, (start, size) in enumerate(CHUNKS):
        here = pl.ds(start, size)
        part = [pltpu.make_async_copy(sum_in.at[here, :], partial.at[here, :], lsem.at[5 * i])]
        for o, opposite in enumerate(((u0, l0), (u1, l1))):
            wide, place = EARLY * BLOCK, o * len(FAR) * BLOCK
            early = left_in.at[here, pl.ds(o * wide, wide)]
            part.append(pltpu.make_async_copy(early, left.at[here, pl.ds(place, wide)], lsem.at[5 * i + 1 + o]))
            target = left.at[here, pl.ds(place + wide, 4 * BLOCK)]
            part.append(pltpu.make_async_copy(opposite[i], target, lsem.at[5 * i + 3 + o]))
        parts.append(part)
    for group in (blocks[:WIDE], parts[0], blocks[WIDE:], *parts[1:]):
        for copy in group:
            copy.start()
    sums = [jnp.zeros((1, BLOCK), F32) for _ in range(ROWS)]
    for i, part in enumerate(parts):
        start, size = CHUNKS[i]
        for copy in part:
            copy.wait()
        for group in range(ROWS // WIDE):
            if i == 0:
                for copy in blocks[WIDE * group:WIDE * group + WIDE]:
                    copy.wait()
            product = jnp.dot(
                left[start:start + size, :],
                far[group].reshape(depth, WIDE * BLOCK),
                preferred_element_type=F32,
            )
            for n in range(WIDE):
                lanes = slice(n * BLOCK, (n + 1) * BLOCK)
                column = WIDE * group + n
                target = slice(column * BLOCK, (column + 1) * BLOCK)
                for j in range(size // BLOCK):
                    keep = cpat_ref[start // BLOCK + j, column] != 0
                    place = slice(start + j * BLOCK, start + (j + 1) * BLOCK)
                    block = product[j * BLOCK:(j + 1) * BLOCK, lanes] + partial[place, target]
                    block = jnp.where(keep, block * block, jnp.zeros_like(block))
                    o_ref[place, target] = block
                    sums[column] = sums[column] + jnp.sum(block, axis=0, keepdims=True)
    for r in range(ROWS):
        for n in range(ROWS):
            t_ref[r, n:n + 1, :] = sums[n]


def cost(rows, sources, data):
    return pl.CostEstimate(
        flops=2 * rows * sources * BLOCK * ROWS * BLOCK, bytes_accessed=data << 20, transcendentals=0
    )


def first_product(lefts, nears):
    rows, sources = 2 * HALF, 2 * EARLY
    return pl.pallas_call(
        first_kernel,
        out_shape=[pltpu.HBM((rows, sources * BLOCK), BF16), pltpu.HBM((rows, ROWS * BLOCK), F32)],
        in_specs=[any_space()] * (len(lefts) + len(nears)),
        out_specs=[any_space()] * 2,
        scratch_shapes=[
            pltpu.VMEM((2, CHUNK, (COLS - 8) * BLOCK), BF16),
            pltpu.VMEM((2, 6, CHUNK, 512), BF16),
            pltpu.VMEM((2 * len(NEAR), BLOCK, ROWS * BLOCK), BF16),
            pltpu.VMEM((2, CHUNK, ROWS * BLOCK), F32),
            pltpu.SemaphoreType.DMA((len(nears),)),
            pltpu.SemaphoreType.DMA((36,)),
            pltpu.SemaphoreType.DMA((12,)),
        ],
        compiler_params=limit(24),
        cost_estimate=cost(rows, 2 * len(NEAR), 32),
    )(*lefts, *[outside(array) for array in nears])


def second_product(cpat, left, opposite, partial, fars):
    rows, depth = 2 * HALF, 2 * len(FAR) * BLOCK
    return pl.pallas_call(
        second_kernel,
        out_shape=[
            pltpu.VMEM((rows, ROWS * BLOCK), F32),
            jax.ShapeDtypeStruct((ROWS, ROWS, BLOCK), F32),
        ],
        in_specs=[smem()] + [any_space()] * 7,
        out_specs=[vmem()] * 2,
        scratch_shapes=[
            pltpu.VMEM((rows, depth), BF16),
            pltpu.VMEM((rows, ROWS * BLOCK), F32),
            pltpu.VMEM((ROWS // WIDE, 2 * len(FAR), BLOCK, WIDE * BLOCK), BF16),
            pltpu.SemaphoreType.DMA((ROWS,)),
            pltpu.SemaphoreType.DMA((10,)),
        ],
        compiler_params=limit(32),
        cost_estimate=cost(rows, 2 * len(FAR), 24),
    )(cpat, outside(left), *opposite, outside(partial), outside(fars))


def rescale_kernel(count, t_ref, i_ref, o_ref):
    total = t_ref[0]
    for r in range(1, ROWS):
        total = total + t_ref[r]
    scale = count / (total + EPS)
    rows = pl.ds(pl.program_id(0) * o_ref.shape[0], o_ref.shape[0])
    for n in range(ROWS):
        lanes = slice(n * BLOCK, (n + 1) * BLOCK)
        o_ref[:, lanes] = (i_ref[rows, lanes] * scale[n:n + 1, :]).astype(BF16)


def rescale(totals, inflated):
    rows, columns = inflated.shape
    tile = 512
    return pl.pallas_call(
        functools.partial(rescale_kernel, float(rows * ROWS)),
        out_shape=jax.ShapeDtypeStruct((rows, columns), BF16),
        grid=(rows // tile,),
        in_specs=[pl.BlockSpec(totals.shape, lambda i: (0, 0, 0)), vmem()],
        out_specs=pl.BlockSpec((tile, columns), lambda i: (i, 0)),
        compiler_params=limit(16),
        cost_estimate=pl.CostEstimate(flops=rows * 2048, bytes_accessed=4 << 20, transcendentals=0),
    )(totals, held(inflated))


def shards(a_values, b_values, a_pattern, b_pattern, c_pattern):
    col = lax.axis_index("col").astype(jnp.int32)
    row = lax.axis_index("row").astype(jnp.int32)
    x, y, c = col >> 3, (col >> 1) & (YS - 1), col & (CORES - 1)

    sent = spread(b_values, b_pattern, row[None])
    received = lax.all_to_all(sent, "col", split_axis=0, concat_axis=0, tiled=True)

    left = mask_left(a_values, a_pattern)
    where = []
    steps = ((0, 0), (1, 0), (-1, 0), (0, 1), (0, -1))
    for first, second in steps:
        there = place(x, y, c, first, second)
        where += [there, there ^ 1]
    near = pieces(b_values, b_pattern, jnp.stack(where))
    index = []
    for core in (c, 1 - c):
        for d, e in FAR:
            index.append(place(x, y, core, OFFSETS[e], OFFSETS[d]))
    received, left, near = lax.optimization_barrier((received, left, near))
    own = select(received, jnp.stack(index))
    left, near, _ = lax.optimization_barrier((left, near, own))

    fars = lax.all_gather(own, "row", axis=0, tiled=True)

    line = jnp.concatenate([left] + [shift(left, s, 0) for s in (1, -1, 2)], axis=1)
    below, above = shift(line, 0, 1), shift(line, 0, -1)
    opposite = [shift(below[:HALF], 0, 1), shift(above[HALF:], 0, -1)]
    lefts = [line, below, above]
    lefts = lefts + [swap(g) for g in lefts]

    nears = [near[0]] + [shift(piece, *step) for piece, step in zip(near[1:], steps[1:])]
    nears.append(swap(jnp.stack([piece[1] for piece in nears])))

    left, partial = first_product(lefts, nears)
    opposite, partial = lax.optimization_barrier((opposite, partial))
    opposite = opposite + [swap(g) for g in opposite]
    inflated, totals = second_product(c_pattern, left, opposite, partial, fars)
    gathered = lax.all_to_all(totals, "row", split_axis=0, concat_axis=0, tiled=True)
    return rescale(gathered, inflated)


def solution(mesh):
    return jax.shard_map(
        shards,
        mesh=mesh,
        in_specs=(
            P("row", "col"),
            P("col", None),
            P("row", "col"),
            P("col", None),
            P("row", "col"),
        ),
        out_specs=P("row", "col"),
        check_vma=False,
    )
```
